128 devices in a mesh: face: 16 (over x, z), col: 8 (over y, core).
Axes of the slice: x: 4, y: 4, z: 4, core: 2. Of those that a mesh axis runs over, the one named last changes fastest.
Arguments:
- prognostic: float32 [5, 128, 32, 1024], P(None, None, 'face', 'col'), may hold values from -6 to 6
- diffusivity: float32 [16, 8, 512, 128], P('face', 'col'), may hold values from 0.05 to 5
- surface_flux: float32 [16, 8, 512], P('face', 'col'), may hold values from -8 to 8
- assignment: int32 [16, 8, 256, 1], P('face', 'col'), may hold values from 0 to 127; in each aligned block of 256 rows (0 to 255, 256 to 511, ..., all dimensions but the last counted through in order) at most 4 rows name the same one
Outputs:
- updated: float32 [5, 128, 32, 1024], P(None, None, 'face', 'col')
The draws below stay inside these ranges and needn't reach their ends.
Inputs may be any that keep to these rules, and one draw needn't show every extreme that they name: `assignment`: among the 256 columns of one device at most 4 have the same owner; some owner gets exactly 4 of them from some device.
All inputs are finite; a program needn't handle non-finite values.
Results may differ from the reference program's by a relative error of at most 0.0003.
Values sent between devices are 32-bit elements; how exact they have to be, the bound alone decides.
A program may use at most 64 MiB of HBM per device.

```python
import math
import jax
import jax.numpy as jnp
import numpy as np
from jax import lax

TILE_Y = 2
TILE_X = 128
LEVELS = 128
FIELDS = 5
COLS_DEV = 256
CAPACITY = 4
OWNER_SLOTS = 512
NY = 32
NX = 1024
N_FACE = 16
N_COL = 8
DEVICES = 128


def block_scale(rng, extent, split, low, top_value):
    gain = 1.0
    for axis_at, parts in split:
        draws = jax.random.uniform(jax.random.fold_in(jax.random.fold_in(rng, 6), axis_at), (parts,), jnp.float32, low / len(split), top_value / len(split))
        gain = gain * jnp.repeat(jnp.exp(draws), extent[axis_at] // parts).reshape((-1,) + (1,) * (len(extent) - 1 - axis_at))
    return gain


def shared_out(stream_key, own, number, rows, amount, top, limit, lean):
    sequence = jax.random.permutation(stream_key, amount)
    crowded, ordinary = shares(amount, rows * top, limit, lean, True), shares(amount, rows * top, limit, lean, False)
    places = jnp.arange(amount)

    def named(sizes, rotation):
        used = int((sizes > 0).sum())
        fixed = max(1, used // 4)
        passed = fixed + (places - fixed + rotation * (used - fixed)) % max(1, amount - fixed)
        return jnp.zeros((amount,), jnp.int32).at[sequence[jnp.where(places < fixed, places, passed)]].set(jnp.asarray(sizes, jnp.int32))

    sizes = jnp.where(number % 4 == 0, named(crowded, number // 4), named(ordinary, number - number // 4 - 1))
    mixed = jax.random.permutation(jax.random.fold_in(own, 3), amount)
    giver, receiver = mixed[0:amount // 2 * 2:2], mixed[1:amount // 2 * 2:2]
    margin = jnp.minimum(sizes[giver] - 1, limit - sizes[receiver]) // 2
    margin = jnp.where((giver == sequence[0]) | (receiver == sequence[0]) | (sizes[receiver] == 0), 0, jnp.maximum(margin, 0))
    passed = jax.random.randint(jax.random.fold_in(own, 4), (amount // 2,), 0, 1 << 20) % (margin + 1)
    sizes = sizes.at[giver].add(-passed).at[receiver].add(passed)
    items = jnp.searchsorted(jnp.cumsum(sizes), jnp.arange(rows * top), side="right").astype(jnp.int32)
    table = items.reshape(top, rows).T
    table = table[jax.random.permutation(jax.random.fold_in(own, 1), rows)]
    rotation = jax.random.randint(jax.random.fold_in(own, 2), (rows, 1), 0, top)
    return jnp.take_along_axis(table, (jnp.arange(top)[None, :] + rotation) % top, axis=1)


def shares(amount, total, reach, skew, full):
    loads = [(1 << 20) // math.isqrt(grade ** skew) + 1 for grade in range(1, amount + 1)]
    largest = reach if full else min(reach, max(-(-total // amount), total * loads[0] // sum(loads)))
    least = 1 if total - largest >= amount - 1 else 0
    counts, spare = [largest] + [least] * (amount - 1), total - largest - least * (amount - 1)
    while spare > 0:
        free = [i for i in range(1, amount) if counts[i] < largest] or [i for i in range(1, amount) if counts[i] < reach]
        whole, left = sum([loads[i] for i in free]), spare
        for i in free:
            addition = min(reach - counts[i], max(1, left * loads[i] // whole), spare)
            counts[i] = counts[i] + addition
            spare = spare - addition
    return np.array(counts)


def normal_values(own_key, shape, deviation, limit, shards=(), kind=jnp.bfloat16):
    entries = jax.random.normal(own_key, shape, jnp.float32) * deviation
    if len(shards) > 0:
        entries = block_scale(own_key, shape, shards, -0.22, 0.18) * entries
    return jnp.clip(entries, min=-limit, max=limit).astype(kind)


def setup_inputs(seed: int = 0) -> dict:
    arg_keys = jax.random.split(jax.random.key(seed), 5)
    prognostic = normal_values(arg_keys[0], (FIELDS, LEVELS, NY, NX), 1.0, 6.0, ((2, 16), (3, 8)), jnp.float32)
    diffusivity = jnp.clip(jnp.exp(math.log(5.0) - 4.6051702 * jax.random.uniform(arg_keys[1], (N_FACE, N_COL, OWNER_SLOTS, LEVELS), jnp.float32) ** block_scale(arg_keys[1], (N_FACE, N_COL, OWNER_SLOTS, LEVELS), ((0, 16), (1, 8)), -0.2, 0.2)), 0.05, 5.0)
    surface_flux = normal_values(arg_keys[2], (N_FACE, N_COL, OWNER_SLOTS), 2.0, 8.0, ((0, 16), (1, 8)), jnp.float32)
    assignment_keys = jax.random.split(jax.random.fold_in(arg_keys[3], 1), N_FACE * N_COL * COLS_DEV // COLS_DEV)
    assignment_turns = jax.random.permutation(jax.random.fold_in(arg_keys[3], 3), N_FACE * N_COL * COLS_DEV // COLS_DEV)
    assignment = jax.vmap(lambda own, number: shared_out(jax.random.fold_in(arg_keys[3], 2), own, number, COLS_DEV, DEVICES, 1, CAPACITY, 2))(assignment_keys, assignment_turns).reshape((N_FACE, N_COL, COLS_DEV, 1))
    return dict(prognostic=prognostic, diffusivity=diffusivity, surface_flux=surface_flux, assignment=assignment)


SMOOTHING = 0.2

def column_solve(columns, kappa, surface):
    levels = kappa.shape[-1]
    fields = columns.shape[-2]
    bottom = (jnp.arange(fields)[:, None] == 0) & (jnp.arange(levels)[None, :] == levels - 1)
    forcing = columns + jnp.where(bottom, surface[..., None, None], 0.0)
    coupling = jnp.concatenate([jnp.zeros_like(kappa[..., :1]), kappa[..., :-1]], axis=-1)
    lower_band = jnp.broadcast_to(-coupling[..., None, :], forcing.shape)
    main_band = jnp.broadcast_to((1.0 + coupling + kappa)[..., None, :], forcing.shape)
    upper_coef = jnp.concatenate([-kappa[..., :-1], jnp.zeros_like(kappa[..., :1])], axis=-1)
    upper_band = jnp.broadcast_to(upper_coef[..., None, :], forcing.shape)
    solved = lax.linalg.tridiagonal_solve(lower_band, main_band, upper_band, forcing[..., None])
    return solved[..., 0]

def reference(prognostic, diffusivity, surface_flux, assignment):
    fields = prognostic.shape[0]
    levels = prognostic.shape[1]
    device_count = N_FACE * N_COL
    column_count = TILE_Y * TILE_X
    columns = prognostic.reshape(fields, levels, N_FACE, TILE_Y, N_COL, TILE_X)
    columns = columns.transpose(2, 4, 3, 5, 0, 1).reshape(device_count, column_count, fields, levels)
    kappa_flat = diffusivity.reshape(device_count, device_count * CAPACITY, levels)
    flux_flat = surface_flux.reshape(device_count, device_count * CAPACITY)
    targets = assignment.reshape(device_count, column_count)

    def per_source(packed):
        source_cols, target, source = packed
        one_hot = target[:, None] == jnp.arange(device_count, dtype=jnp.int32)[None, :]
        running = jnp.cumsum(one_hot.astype(jnp.int32), axis=0) - 1
        slot_rank = jnp.sum(jnp.where(one_hot, running, 0), axis=1).astype(jnp.int32)
        slot_index = (source * CAPACITY + slot_rank).astype(jnp.int32)
        kappa_local = kappa_flat[target, slot_index]
        flux_local = flux_flat[target, slot_index]
        return column_solve(source_cols, kappa_local, flux_local)
    solved = lax.map(per_source, (columns, targets, jnp.arange(device_count, dtype=jnp.int32)))
    tendency = solved - columns
    grid_tendency = tendency.reshape(N_FACE, N_COL, TILE_Y, TILE_X, fields, levels)
    grid_tendency = grid_tendency.transpose(4, 5, 0, 2, 1, 3).reshape(prognostic.shape)
    beside_all = jnp.roll(prognostic, 1, axis=2) + jnp.roll(prognostic, -1, axis=2)
    beside_all = beside_all + jnp.roll(prognostic, 1, axis=3) + jnp.roll(prognostic, -1, axis=3)
    laplace = beside_all - 4.0 * prognostic
    return prognostic + grid_tendency + SMOOTHING * laplace
```

```python
import functools

import jax
import jax.numpy as jnp
from jax import lax
from jax.experimental import pallas as pl
from jax.experimental.pallas import tpu as pltpu
from jax.sharding import PartitionSpec as P

MESH = pl.DeviceIdType.MESH
SMOOTHING = 0.2
FACES, COLS = 16, 8
CHIPS = 64
FIELDS, LEVELS, LANES = 5, 128, 128
BLOCKS, STEPS = 8, 16
ROWS = 10
ROOT = FACES - 1
F32, BF16 = jnp.float32, jnp.bfloat16


def split2(value):
    high = value.astype(BF16)
    return high, (value - high.astype(F32)).astype(BF16)


def lookup(table, hot):
    dims = (((0,), (0,)), ((), ()))
    high, low = split2(table)
    return lax.dot_general(high, hot, dims, preferred_element_type=F32) + lax.dot_general(
        low, hot, dims, preferred_element_type=F32
    )


def kernel(
    x_hbm, k_hbm, flux_hbm, assign_hbm, out_hbm,
    xin, target, small, buf, recv, halo, packed, base, work, edge_out, edge_in, hot, kappa_t, out,
    local_sem, swap_send, swap_recv, halo_send, halo_recv, edge_send, edge_recv, all_send, all_recv, out_sem, go_sem,
):
    f, c = lax.axis_index("face"), lax.axis_index("col")
    y, core = c >> 1, c & 1
    chip = f * 4 + y
    up, down = (f + 1) & 15, (f + 15) & 15
    partner = (f, c ^ 1)
    is_root = f == ROOT

    barrier = pltpu.get_barrier_semaphore()
    for r in range(COLS):
        @pl.when(jnp.logical_not(is_root & (c == r)))
        def _():
            pl.semaphore_signal(barrier, inc=1, device_id=(ROOT, r), device_id_type=MESH)
    for peer in ((up, c), (down, c), partner):
        pl.semaphore_signal(barrier, inc=1, device_id=peer, device_id_type=MESH)

    local = [
        pltpu.make_async_copy(x_hbm, xin, local_sem.at[0]),
        pltpu.make_async_copy(assign_hbm, target, local_sem.at[1]),
        pltpu.make_async_copy(k_hbm.at[:, core], buf.at[:, pl.ds(4 * core, 4)], local_sem.at[2]),
        pltpu.make_async_copy(flux_hbm, small.at[core], local_sem.at[3]),
    ]
    for copy in local:
        copy.start()

    @pl.when(is_root)
    def _():
        pl.semaphore_wait(barrier, 3 + FACES * COLS - 1)
        for i in range(FACES - 1):
            pl.semaphore_signal(go_sem, inc=1, device_id=(i, c), device_id_type=MESH)

    @pl.when(jnp.logical_not(is_root))
    def _():
        pl.semaphore_wait(barrier, 3)

    swaps = [
        pltpu.make_async_remote_copy(
            src_ref=src, dst_ref=dst, send_sem=swap_send.at[i], recv_sem=swap_recv.at[i],
            device_id=partner, device_id_type=MESH,
        )
        for i, (src, dst) in enumerate((
            (k_hbm.at[:, 1 - core], buf.at[:, pl.ds(4 * core, 4)]),
            (flux_hbm, small.at[core]),
        ))
    ]
    for copy in swaps:
        copy.start()

    halos = []
    for fl in range(FIELDS):
        at = pl.ds(fl * LEVELS, LEVELS)
        for d, row, peer in ((0, 1, up), (1, 0, down)):
            copy = pltpu.make_async_remote_copy(
                src_ref=x_hbm.at[at, row], dst_ref=halo.at[d, at],
                send_sem=halo_send.at[d, fl], recv_sem=halo_recv.at[d, fl],
                device_id=(peer, c), device_id_type=MESH,
            )
            copy.start()
            halos.append(copy)

    lane = lax.broadcasted_iota(jnp.int32, (8, LANES), 1)
    sub = lax.broadcasted_iota(jnp.int32, (8, LANES), 0)
    local[0].wait()
    x_rows = xin.reshape(FIELDS * LEVELS * 2, LANES)

    def pack(fl, edges):
        edges = list(edges)
        for j in range(STEPS):
            i = fl * STEPS + j
            for r in range(2):
                p = x_rows[pl.ds(fl * 2 * LEVELS + 2 * j + r, BLOCKS, stride=2 * STEPS), :]
                packed[r, fl, j] = p
                edges[r] = jnp.where(lane == i, pltpu.roll(p, i + 1, axis=1), edges[r])
                edges[2 + r] = jnp.where(lane == i, pltpu.roll(p, i, axis=1), edges[2 + r])
        return tuple(edges)

    edges = lax.fori_loop(0, FIELDS, pack, tuple(jnp.zeros((8, LANES), F32) for _ in range(4)))
    for n in range(4):
        edge_out[n // 2, n % 2] = edges[n]

    local[2].wait()
    local[3].wait()
    for copy in swaps:
        copy.wait_recv()
    for s in range(2):
        for g in range(4):
            buf[pl.ds(16 * g, 16), 8 + s] = jnp.broadcast_to(small[s, g], (16, 1, LANES))

    @pl.when(jnp.logical_not(is_root))
    def _():
        pl.semaphore_wait(go_sem, 1)

    for i in range(1, CHIPS):
        pf, py = (f + (i >> 2)) & 15, (y + (i & 3)) & 3
        pltpu.make_async_remote_copy(
            src_ref=buf.at[pf * 4 + py], dst_ref=recv.at[chip], send_sem=all_send, recv_sem=all_recv,
            device_id=(pf, py * 2 + core), device_id_type=MESH,
        ).start()
    own = pltpu.make_async_copy(buf.at[chip], recv.at[chip], local_sem.at[4])
    own.start()
    edge_copies = [
        pltpu.make_async_remote_copy(
            src_ref=edge_out.at[n], dst_ref=edge_in.at[n], send_sem=edge_send.at[n], recv_sem=edge_recv.at[n],
            device_id=(f, (c + step) & 7), device_id_type=MESH,
        )
        for n, step in ((0, 1), (1, 7))
    ]
    for copy in edge_copies:
        copy.start()

    local[1].wait()
    t = target[...]
    owner_hot = (lax.broadcasted_iota(jnp.int32, (FACES * COLS, 256), 0) == t).astype(F32)
    before = (
        lax.broadcasted_iota(jnp.int32, (256, 256), 0) < lax.broadcasted_iota(jnp.int32, (256, 256), 1)
    ).astype(F32)
    running = jnp.dot(owner_hot.astype(BF16), before.astype(BF16), preferred_element_type=F32)
    rank = jnp.sum(owner_hot * running, axis=0, keepdims=True)
    row = ((t >> 1) * ROWS + (t & 1) * 4).astype(F32) + rank
    slots = lax.broadcasted_iota(jnp.int32, (CHIPS * ROWS, 256), 0).astype(F32)
    hot[...] = (slots == row).astype(F32).astype(BF16)

    for copy in edge_copies:
        copy.wait_recv()

    def smooth(fl, carry):
        for j in range(STEPS):
            i = fl * STEPS + j
            for r in range(2):
                p = packed[r, fl, j]
                left = jnp.where(lane == 0, pltpu.roll(edge_in[0, r], LANES - i, axis=1), pltpu.roll(p, 1, axis=1))
                right = jnp.where(
                    lane == LANES - 1,
                    pltpu.roll(edge_in[1, r], LANES - 1 - i, axis=1),
                    pltpu.roll(p, LANES - 1, axis=1),
                )
                base[r, fl, j] = SMOOTHING * (packed[1 - r, fl, j] + left + right - 4.0 * p)
        return carry

    lax.fori_loop(0, FIELDS, smooth, 0)

    own.wait()
    pltpu.make_async_copy(recv.at[pl.ds(0, CHIPS - 1)], recv.at[pl.ds(0, CHIPS - 1)], all_recv).wait()
    received = recv.reshape(CHIPS * ROWS, LANES)
    columns = lookup(received[...], hot[...])
    kappa_t[0] = columns[:, :LANES]
    kappa_t[1] = columns[:, LANES:]
    flux_rows = jnp.concatenate(
        [received[pl.ds(8, CHIPS, stride=ROWS), :], received[pl.ds(9, CHIPS, stride=ROWS), :]], axis=0
    )
    flux_hot = (
        lax.broadcasted_iota(jnp.int32, (FACES * COLS, 256), 0) == (t >> 1) + (t & 1) * CHIPS
    ).astype(F32)
    flux = lookup(flux_rows, flux_hot.astype(BF16))
    wanted = rank + ((f & 3) * 32 + c * 4).astype(F32)
    lanes_at = lax.broadcasted_iota(jnp.int32, (LANES, 256), 0).astype(F32)
    heat = jnp.sum(jnp.where(lanes_at == wanted, flux, 0.0), axis=0, keepdims=True)
    heat = [jnp.where(sub == BLOCKS - 1, heat[:, r * LANES : (r + 1) * LANES], 0.0) for r in range(2)]

    def interface(j):
        return jnp.stack([kappa_t[r, pl.ds(j, BLOCKS, stride=STEPS), :] for r in range(2)])

    subs = jnp.stack([sub, sub])
    ks = [interface(j) for j in range(STEPS)]
    last = jnp.where(subs == BLOCKS - 1, 0.0, ks[-1])
    above = jnp.where(subs == 0, 0.0, pltpu.roll(ks[-1], 1, axis=1))
    q = 1.0 + above
    u = above
    d = packed[:, :, 0]
    work[:, :, 0] = d
    us, rps, gs = [u], [], []
    for j in range(1, STEPS + 1):
        k = ks[j - 1]
        pivot = q + k
        if j == STEPS:
            break
        rp = 1.0 / pivot
        g = k * rp
        q = 1.0 + (k * q) * rp
        d = packed[:, :, j] + g[:, None] * d
        u = g * u
        if j == STEPS - 1:
            d = jnp.concatenate([(d[:, :1] + jnp.stack(heat)[:, None]), d[:, 1:]], axis=1)
        else:
            work[:, :, j] = d
        us.append(u)
        rps.append(rp)
        gs.append(g)
    v = rps[-1][:, None] * work[:, :, STEPS - 2]
    w = gs[-1]
    u0 = rps[-1] * us[STEPS - 2]
    work[:, :, STEPS - 2] = v
    u_all, w_all = [None] * STEPS, [None] * STEPS
    u_all[STEPS - 2], w_all[STEPS - 2] = u0, w
    for j in range(STEPS - 3, -1, -1):
        v = rps[j][:, None] * work[:, :, j] + gs[j][:, None] * v
        u0 = rps[j] * us[j] + gs[j] * u0
        w = gs[j] * w
        work[:, :, j] = v
        u_all[j], w_all[j] = u0, w

    def prev(value, n=1):
        return pltpu.roll(value, n, axis=value.ndim - 2)

    def following(value, n=1):
        return pltpu.roll(value, BLOCKS - n, axis=value.ndim - 2)

    inverse = 1.0 / (pivot - last * following(u0))
    a = us[STEPS - 1] * inverse
    b = last * following(w) * inverse
    rhs = (d + last[:, None] * following(v)) * inverse[:, None]
    for n in (1, 2, 4):
        inverse = 1.0 / (1.0 - a * prev(b, n) - b * following(a, n))
        rhs = (rhs + a[:, None] * prev(rhs, n) + b[:, None] * following(rhs, n)) * inverse[:, None]
        a, b = a * prev(a, n) * inverse, b * following(b, n) * inverse
    bottom = rhs
    top = jnp.where(subs[:, None] == 0, 0.0, prev(bottom))
    for j in range(STEPS - 1):
        base[:, :, j] += work[:, :, j] + u_all[j][:, None] * top + w_all[j][:, None] * bottom
    base[:, :, STEPS - 1] += bottom

    halo_rows = halo.reshape(2 * FIELDS * LEVELS, LANES)
    out_rows = out.reshape(FIELDS * LEVELS * 2, LANES)
    outs = []
    for fl in range(FIELDS):
        for d_at in range(2):
            halos[2 * fl + d_at].wait_recv()
        for j in range(STEPS):
            for r in range(2):
                beside = halo_rows[pl.ds((r * FIELDS + fl) * LEVELS + j, BLOCKS, stride=STEPS), :]
                out_rows[pl.ds(fl * 2 * LEVELS + 2 * j + r, BLOCKS, stride=2 * STEPS), :] = (
                    base[r, fl, j] + SMOOTHING * beside
                )
        at = pl.ds(fl * LEVELS, LEVELS)
        copy = pltpu.make_async_copy(out.at[at], out_hbm.at[at], out_sem.at[fl])
        copy.start()
        outs.append(copy)

    pltpu.make_async_copy(recv.at[pl.ds(0, CHIPS - 1)], recv.at[pl.ds(0, CHIPS - 1)], all_send).wait()
    for copy in swaps + edge_copies + halos:
        copy.wait_send()
    for copy in outs:
        copy.wait()


def shards(prognostic, diffusivity, surface_flux, assignment):
    x = prognostic.reshape(FIELDS * LEVELS, 2, 1, LANES)
    k = diffusivity.reshape(CHIPS, 2, 4, 1, LEVELS)
    flux = surface_flux.reshape(4, 1, LANES)
    target = assignment.reshape(1, 256)
    any_spec = pl.BlockSpec(memory_space=pl.ANY)
    dma = pltpu.SemaphoreType.DMA
    wide = (2, FIELDS, STEPS, BLOCKS, LANES)
    result = pl.pallas_call(
        kernel,
        out_shape=jax.ShapeDtypeStruct(x.shape, F32),
        in_specs=[any_spec] * 4,
        out_specs=any_spec,
        scratch_shapes=[
            pltpu.VMEM(x.shape, F32),
            pltpu.VMEM((1, 256), jnp.int32),
            pltpu.VMEM((2, 4, 1, LANES), F32),
            pltpu.VMEM((CHIPS, ROWS, 1, LANES), F32),
            pltpu.VMEM((CHIPS, ROWS, 1, LANES), F32),
            pltpu.VMEM((2, FIELDS * LEVELS, 1, LANES), F32),
            pltpu.VMEM(wide, F32),
            pltpu.VMEM(wide, F32),
            pltpu.VMEM(wide, F32),
            pltpu.VMEM((2, 2, BLOCKS, LANES), F32),
            pltpu.VMEM((2, 2, BLOCKS, LANES), F32),
            pltpu.VMEM((CHIPS * ROWS, 256), BF16),
            pltpu.VMEM((2, LEVELS, LANES), F32),
            pltpu.VMEM(x.shape, F32),
            dma((5,)),
            dma((2,)),
            dma((2,)),
            dma((2, FIELDS)),
            dma((2, FIELDS)),
            dma((2,)),
            dma((2,)),
            dma,
            dma,
            dma((FIELDS,)),
            pltpu.SemaphoreType.REGULAR,
        ],
        compiler_params=pltpu.CompilerParams(
            collective_id=0, has_side_effects=True, vmem_limit_bytes=56 << 20
        ),
    )(x, k, flux, target)
    return result.reshape(prognostic.shape)


def solution(mesh):
    return jax.shard_map(
        shards,
        mesh=mesh,
        in_specs=(
            P(None, None, "face", "col"),
            P("face", "col", None, None),
            P("face", "col", None),
            P("face", "col", None, None),
        ),
        out_specs=P(None, None, "face", "col"),
        check_vma=False,
    )
```

```python
import functools

import jax
import jax.numpy as jnp
from jax import lax
from jax.experimental import pallas as pl
from jax.experimental.pallas import tpu as pltpu
from jax.sharding import PartitionSpec as P

MESH = pl.DeviceIdType.MESH
SMOOTHING = 0.2
FACES, COLS = 16, 8
CHIPS = 64
FIELDS, LEVELS, LANES = 5, 128, 128
BLOCKS, STEPS = 8, 16
ROWS = 10
ROOT = 13
F32, BF16 = jnp.float32, jnp.bfloat16


def split2(value):
    high = value.astype(BF16)
    return high, (value - high.astype(F32)).astype(BF16)


def lookup(table, hot):
    dims = (((0,), (0,)), ((), ()))
    high, low = split2(table)
    return lax.dot_general(high, hot, dims, preferred_element_type=F32) + lax.dot_general(
        low, hot, dims, preferred_element_type=F32
    )


def kernel(
    x_hbm, k_hbm, flux_hbm, assign_hbm, out,
    xin, target, small, buf, recv, halo, packed, base, work, edge_out, edge_in, hot, kappa_t,
    local_sem, swap_send, swap_recv, halo_send, halo_recv, edge_send, edge_recv, all_send, all_recv, go_sem,
):
    f, c = lax.axis_index("face"), lax.axis_index("col")
    y, core = c >> 1, c & 1
    chip = f * 4 + y
    up, down = (f + 1) & 15, (f + 15) & 15
    partner = (f, c ^ 1)
    is_root = f == ROOT

    barrier = pltpu.get_barrier_semaphore()
    for r in range(COLS):
        @pl.when(jnp.logical_not(is_root & (c == r)))
        def _():
            pl.semaphore_signal(barrier, inc=1, device_id=(ROOT, r), device_id_type=MESH)
    for peer in ((up, c), (down, c), partner):
        pl.semaphore_signal(barrier, inc=1, device_id=peer, device_id_type=MESH)

    local = [
        pltpu.make_async_copy(x_hbm, xin, local_sem.at[0]),
        pltpu.make_async_copy(assign_hbm, target, local_sem.at[1]),
        pltpu.make_async_copy(k_hbm.at[:, core], buf.at[:, pl.ds(4 * core, 4)], local_sem.at[2]),
        pltpu.make_async_copy(flux_hbm, small.at[core], local_sem.at[3]),
    ]
    for copy in local:
        copy.start()

    @pl.when(is_root)
    def _():
        pl.semaphore_wait(barrier, 3 + FACES * COLS - 1)
        for i in [j for j in range(FACES) if j != ROOT]:
            pl.semaphore_signal(go_sem, inc=1, device_id=(i, c), device_id_type=MESH)

    @pl.when(jnp.logical_not(is_root))
    def _():
        pl.semaphore_wait(barrier, 3)

    swaps = [
        pltpu.make_async_remote_copy(
            src_ref=src, dst_ref=dst, send_sem=swap_send.at[i], recv_sem=swap_recv.at[i],
            device_id=partner, device_id_type=MESH,
        )
        for i, (src, dst) in enumerate((
            (k_hbm.at[:, 1 - core], buf.at[:, pl.ds(4 * core, 4)]),
            (flux_hbm, small.at[core]),
        ))
    ]
    for copy in swaps:
        copy.start()

    halos = []
    for fl in range(FIELDS):
        at = pl.ds(fl * LEVELS, LEVELS)
        for d, row, peer in ((0, 1, up), (1, 0, down)):
            copy = pltpu.make_async_remote_copy(
                src_ref=x_hbm.at[at, row], dst_ref=halo.at[d, at],
                send_sem=halo_send.at[d, fl], recv_sem=halo_recv.at[d, fl],
                device_id=(peer, c), device_id_type=MESH,
            )
            copy.start()
            halos.append(copy)

    lane = lax.broadcasted_iota(jnp.int32, (8, LANES), 1)
    sub = lax.broadcasted_iota(jnp.int32, (8, LANES), 0)
    local[0].wait()
    x_rows = xin.reshape(FIELDS * LEVELS * 2, LANES)

    def pack(fl, edges):
        edges = list(edges)
        for j in range(STEPS):
            i = fl * STEPS + j
            for r in range(2):
                p = x_rows[pl.ds(fl * 2 * LEVELS + 2 * j + r, BLOCKS, stride=2 * STEPS), :]
                packed[r, fl, j] = p
                edges[r] = jnp.where(lane == i, pltpu.roll(p, i + 1, axis=1), edges[r])
                edges[2 + r] = jnp.where(lane == i, pltpu.roll(p, i, axis=1), edges[2 + r])
        return tuple(edges)

    edges = lax.fori_loop(0, FIELDS, pack, tuple(jnp.zeros((8, LANES), F32) for _ in range(4)))
    for n in range(4):
        edge_out[n // 2, n % 2] = edges[n]

    local[2].wait()
    local[3].wait()
    for copy in swaps:
        copy.wait_recv()
    for s in range(2):
        for g in range(4):
            buf[pl.ds(16 * g, 16), 8 + s] = jnp.broadcast_to(small[s, g], (16, 1, LANES))

    @pl.when(jnp.logical_not(is_root))
    def _():
        pl.semaphore_wait(go_sem, 1)

    for i in range(1, CHIPS):
        pf, py = (f + (i >> 2)) & 15, (y + (i & 3)) & 3
        pltpu.make_async_remote_copy(
            src_ref=buf.at[pf * 4 + py], dst_ref=recv.at[chip], send_sem=all_send, recv_sem=all_recv,
            device_id=(pf, py * 2 + core), device_id_type=MESH,
        ).start()
    own = pltpu.make_async_copy(buf.at[chip], recv.at[chip], local_sem.at[4])
    own.start()
    edge_copies = [
        pltpu.make_async_remote_copy(
            src_ref=edge_out.at[n], dst_ref=edge_in.at[n], send_sem=edge_send.at[n], recv_sem=edge_recv.at[n],
            device_id=(f, (c + step) & 7), device_id_type=MESH,
        )
        for n, step in ((0, 1), (1, 7))
    ]
    for copy in edge_copies:
        copy.start()

    local[1].wait()
    t = target[...]
    owner_hot = (lax.broadcasted_iota(jnp.int32, (FACES * COLS, 256), 0) == t).astype(F32)
    before = (
        lax.broadcasted_iota(jnp.int32, (256, 256), 0) < lax.broadcasted_iota(jnp.int32, (256, 256), 1)
    ).astype(F32)
    running = jnp.dot(owner_hot.astype(BF16), before.astype(BF16), preferred_element_type=F32)
    rank = jnp.sum(owner_hot * running, axis=0, keepdims=True)
    row = ((t >> 1) * ROWS + (t & 1) * 4).astype(F32) + rank
    slots = lax.broadcasted_iota(jnp.int32, (CHIPS * ROWS, 256), 0).astype(F32)
    hot[...] = (slots == row).astype(F32).astype(BF16)

    for copy in edge_copies:
        copy.wait_recv()

    def smooth(fl, carry):
        for j in range(STEPS):
            i = fl * STEPS + j
            for r in range(2):
                p = packed[r, fl, j]
                left = jnp.where(lane == 0, pltpu.roll(edge_in[0, r], LANES - i, axis=1), pltpu.roll(p, 1, axis=1))
                right = jnp.where(
                    lane == LANES - 1,
                    pltpu.roll(edge_in[1, r], LANES - 1 - i, axis=1),
                    pltpu.roll(p, LANES - 1, axis=1),
                )
                base[r, fl, j] = SMOOTHING * (packed[1 - r, fl, j] + left + right - 4.0 * p)
        return carry

    lax.fori_loop(0, FIELDS, smooth, 0)

    own.wait()
    pltpu.make_async_copy(recv.at[pl.ds(0, CHIPS - 1)], recv.at[pl.ds(0, CHIPS - 1)], all_recv).wait()
    received = recv.reshape(CHIPS * ROWS, LANES)
    columns = lookup(received[...], hot[...])
    kappa_t[0] = columns[:, :LANES]
    kappa_t[1] = columns[:, LANES:]
    flux_rows = jnp.concatenate(
        [received[pl.ds(8, CHIPS, stride=ROWS), :], received[pl.ds(9, CHIPS, stride=ROWS), :]], axis=0
    )
    flux_hot = (
        lax.broadcasted_iota(jnp.int32, (FACES * COLS, 256), 0) == (t >> 1) + (t & 1) * CHIPS
    ).astype(F32)
    flux = lookup(flux_rows, flux_hot.astype(BF16))
    wanted = rank + ((f & 3) * 32 + c * 4).astype(F32)
    lanes_at = lax.broadcasted_iota(jnp.int32, (LANES, 256), 0).astype(F32)
    heat = jnp.sum(jnp.where(lanes_at == wanted, flux, 0.0), axis=0, keepdims=True)
    heat = [jnp.where(sub == BLOCKS - 1, heat[:, r * LANES : (r + 1) * LANES], 0.0) for r in range(2)]

    def interface(j):
        return jnp.stack([kappa_t[r, pl.ds(j, BLOCKS, stride=STEPS), :] for r in range(2)])

    subs = jnp.stack([sub, sub])
    ks = [interface(j) for j in range(STEPS)]
    last = jnp.where(subs == BLOCKS - 1, 0.0, ks[-1])
    above = jnp.where(subs == 0, 0.0, pltpu.roll(ks[-1], 1, axis=1))
    q = 1.0 + above
    u = above
    d = packed[:, :, 0]
    work[:, :, 0] = d
    us, rps, gs = [u], [], []
    for j in range(1, STEPS + 1):
        k = ks[j - 1]
        pivot = q + k
        if j == STEPS:
            break
        rp = 1.0 / pivot
        g = k * rp
        q = 1.0 + (k * q) * rp
        d = packed[:, :, j] + g[:, None] * d
        u = g * u
        if j == STEPS - 1:
            d = jnp.concatenate([(d[:, :1] + jnp.stack(heat)[:, None]), d[:, 1:]], axis=1)
        else:
            work[:, :, j] = d
        us.append(u)
        rps.append(rp)
        gs.append(g)
    v = rps[-1][:, None] * work[:, :, STEPS - 2]
    w = gs[-1]
    u0 = rps[-1] * us[STEPS - 2]
    work[:, :, STEPS - 2] = v
    u_all, w_all = [None] * STEPS, [None] * STEPS
    u_all[STEPS - 2], w_all[STEPS - 2] = u0, w
    for j in range(STEPS - 3, -1, -1):
        v = rps[j][:, None] * work[:, :, j] + gs[j][:, None] * v
        u0 = rps[j] * us[j] + gs[j] * u0
        w = gs[j] * w
        work[:, :, j] = v
        u_all[j], w_all[j] = u0, w

    def prev(value, n=1):
        return pltpu.roll(value, n, axis=value.ndim - 2)

    def following(value, n=1):
        return pltpu.roll(value, BLOCKS - n, axis=value.ndim - 2)

    inverse = 1.0 / (pivot - last * following(u0))
    a = us[STEPS - 1] * inverse
    b = last * following(w) * inverse
    rhs = (d + last[:, None] * following(v)) * inverse[:, None]
    for n in (1, 2, 4):
        inverse = 1.0 / (1.0 - a * prev(b, n) - b * following(a, n))
        rhs = (rhs + a[:, None] * prev(rhs, n) + b[:, None] * following(rhs, n)) * inverse[:, None]
        a, b = a * prev(a, n) * inverse, b * following(b, n) * inverse
    bottom = rhs
    top = jnp.where(subs[:, None] == 0, 0.0, prev(bottom))
    for j in range(STEPS - 1):
        base[:, :, j] += work[:, :, j] + u_all[j][:, None] * top + w_all[j][:, None] * bottom
    base[:, :, STEPS - 1] += bottom

    halo_rows = halo.reshape(2 * FIELDS * LEVELS, LANES)
    out_rows = out.reshape(FIELDS * LEVELS * 2, LANES)
    outs = []
    for fl in range(FIELDS):
        for d_at in range(2):
            halos[2 * fl + d_at].wait_recv()
        for j in range(STEPS):
            for r in range(2):
                beside = halo_rows[pl.ds((r * FIELDS + fl) * LEVELS + j, BLOCKS, stride=STEPS), :]
                out_rows[pl.ds(fl * 2 * LEVELS + 2 * j + r, BLOCKS, stride=2 * STEPS), :] = (
                    base[r, fl, j] + SMOOTHING * beside
                )
    pltpu.make_async_copy(recv.at[pl.ds(0, CHIPS - 1)], recv.at[pl.ds(0, CHIPS - 1)], all_send).wait()
    for copy in swaps + edge_copies + halos:
        copy.wait_send()
    for copy in outs:
        copy.wait()


def shards(prognostic, diffusivity, surface_flux, assignment):
    x = prognostic.reshape(FIELDS * LEVELS, 2, 1, LANES)
    k = diffusivity.reshape(CHIPS, 2, 4, 1, LEVELS)
    flux = surface_flux.reshape(4, 1, LANES)
    target = assignment.reshape(1, 256)
    any_spec = pl.BlockSpec(memory_space=pl.ANY)
    dma = pltpu.SemaphoreType.DMA
    wide = (2, FIELDS, STEPS, BLOCKS, LANES)
    result = pl.pallas_call(
        kernel,
        out_shape=pltpu.VMEM(x.shape, F32),
        name="exchange",
        in_specs=[any_spec] * 4,
        out_specs=pl.BlockSpec(memory_space=pltpu.VMEM),
        scratch_shapes=[
            pltpu.VMEM(x.shape, F32),
            pltpu.VMEM((1, 256), jnp.int32),
            pltpu.VMEM((2, 4, 1, LANES), F32),
            pltpu.VMEM((CHIPS, ROWS, 1, LANES), F32),
            pltpu.VMEM((CHIPS, ROWS, 1, LANES), F32),
            pltpu.VMEM((2, FIELDS * LEVELS, 1, LANES), F32),
            pltpu.VMEM(wide, F32),
            pltpu.VMEM(wide, F32),
            pltpu.VMEM(wide, F32),
            pltpu.VMEM((2, 2, BLOCKS, LANES), F32),
            pltpu.VMEM((2, 2, BLOCKS, LANES), F32),
            pltpu.VMEM((CHIPS * ROWS, 256), BF16),
            pltpu.VMEM((2, LEVELS, LANES), F32),
            dma((5,)),
            dma((2,)),
            dma((2,)),
            dma((2, FIELDS)),
            dma((2, FIELDS)),
            dma((2,)),
            dma((2,)),
            dma,
            dma,
            pltpu.SemaphoreType.REGULAR,
        ],
        compiler_params=pltpu.CompilerParams(
            collective_id=0, has_side_effects=True, vmem_limit_bytes=56 << 20
        ),
    )(x, k, flux, target)
    return result.reshape(prognostic.shape)


def solution(mesh):
    return jax.shard_map(
        shards,
        mesh=mesh,
        in_specs=(
            P(None, None, "face", "col"),
            P("face", "col", None, None),
            P("face", "col", None),
            P("face", "col", None, None),
        ),
        out_specs=P(None, None, "face", "col"),
        check_vma=False,
    )
```

```python
import functools

import jax
import jax.numpy as jnp
from jax import lax
from jax.experimental import pallas as pl
from jax.experimental.pallas import tpu as pltpu
from jax.sharding import PartitionSpec as P

MESH = pl.DeviceIdType.MESH
SMOOTHING = 0.2
FACES, COLS = 16, 8
CHIPS = 64
FIELDS, LEVELS, LANES = 5, 128, 128
BLOCKS, STEPS = 8, 16
ROWS = 9
ROOT = 12
ORDER = range(1, CHIPS)
F32, BF16 = jnp.float32, jnp.bfloat16


def split2(value):
    high = value.astype(BF16)
    return high, (value - high.astype(F32)).astype(BF16)


def lookup(table, hot):
    dims = (((0,), (0,)), ((), ()))
    high, low = split2(table)
    return lax.dot_general(high, hot, dims, preferred_element_type=F32) + lax.dot_general(
        low, hot, dims, preferred_element_type=F32
    )


def kernel(
    x_hbm, k_hbm, flux_hbm, assign_hbm, out,
    xin, target, small, buf, recv, halo, packed, base, work, edge_out, edge_in, hot, kappa_t,
    local_sem, swap_send, swap_recv, halo_send, halo_recv, edge_send, edge_recv, all_send, all_recv,
    go_sem, up_sem, down_sem,
):
    f, c = lax.axis_index("face"), lax.axis_index("col")
    y, core = c >> 1, c & 1
    chip = f * 4 + y
    up, down = (f + 1) & 15, (f + 15) & 15
    partner = (f, c ^ 1)
    is_root = f == ROOT

    z = f & 3
    barrier = pltpu.get_barrier_semaphore()
    for r in range(COLS):
        @pl.when(jnp.logical_not(is_root & (c == r)))
        def _():
            pl.semaphore_signal(barrier, inc=1, device_id=(ROOT, r), device_id_type=MESH)
    pl.semaphore_signal(barrier, inc=1, device_id=partner, device_id_type=MESH)

    @pl.when(z != 3)
    def _():
        pl.semaphore_signal(barrier, inc=1, device_id=(up, c), device_id_type=MESH)

    @pl.when(z == 0)
    def _():
        pl.semaphore_signal(barrier, inc=1, device_id=(down, c), device_id_type=MESH)

    local = [
        pltpu.make_async_copy(x_hbm, xin, local_sem.at[0]),
        pltpu.make_async_copy(assign_hbm, target, local_sem.at[1]),
        pltpu.make_async_copy(k_hbm.at[:, core], buf.at[:, pl.ds(4 * core, 4)], local_sem.at[2]),
        pltpu.make_async_copy(flux_hbm, small.at[core], local_sem.at[3]),
    ]
    for copy in local:
        copy.start()

    swaps = [
        pltpu.make_async_remote_copy(
            src_ref=src, dst_ref=dst, send_sem=swap_send.at[i], recv_sem=swap_recv.at[i],
            device_id=partner, device_id_type=MESH,
        )
        for i, (src, dst) in enumerate((
            (k_hbm.at[:, 1 - core], buf.at[:, pl.ds(4 * core, 4)]),
            (flux_hbm, small.at[core]),
        ))
    ]
    halos = [
        [
            pltpu.make_async_remote_copy(
                src_ref=x_hbm.at[pl.ds(fl * LEVELS, LEVELS), row], dst_ref=halo.at[d, pl.ds(fl * LEVELS, LEVELS)],
                send_sem=halo_send.at[d, fl], recv_sem=halo_recv.at[d, fl],
                device_id=(peer, c), device_id_type=MESH,
            )
            for fl in range(FIELDS)
        ]
        for d, row, peer in ((0, 1, up), (1, 0, down))
    ]

    @pl.when(jnp.logical_not(is_root))
    def _():
        @pl.when((z == 1) | (z == 2))
        def _():
            pl.semaphore_wait(barrier, 2)

        @pl.when(z == 3)
        def _():
            pl.semaphore_wait(barrier, 3)

        @pl.when(z == 0)
        def _():
            pl.semaphore_wait(barrier, 1)

        for copy in swaps:
            copy.start()

    @pl.when(z == 3)
    def _():
        pl.semaphore_signal(down_sem, inc=1, device_id=(up, c), device_id_type=MESH)

    @pl.when(z != 0)
    def _():
        pl.semaphore_signal(up_sem, inc=1, device_id=(down, c), device_id_type=MESH)
        for copy in halos[1][:3]:
            copy.start()

    @pl.when(z != 3)
    def _():
        pl.semaphore_wait(up_sem, 1)

    for copy in halos[0][:3]:
        copy.start()

    @pl.when(z == 0)
    def _():
        pl.semaphore_wait(down_sem, 1)
        for copy in halos[1][:3]:
            copy.start()

    @pl.when(is_root)
    def _():
        pl.semaphore_wait(barrier, FACES * COLS)
        for i in [n for n in range(FACES) if n != ROOT]:
            pl.semaphore_signal(go_sem, inc=1, device_id=(i, c), device_id_type=MESH)
        for copy in swaps:
            copy.start()

    lane = lax.broadcasted_iota(jnp.int32, (8, LANES), 1)
    sub = lax.broadcasted_iota(jnp.int32, (8, LANES), 0)
    local[0].wait()
    x_rows = xin.reshape(FIELDS * LEVELS * 2, LANES)

    def pack(fl, edges):
        edges = list(edges)
        for j in range(STEPS):
            i = fl * STEPS + j
            for r in range(2):
                p = x_rows[pl.ds(fl * 2 * LEVELS + 2 * j + r, BLOCKS, stride=2 * STEPS), :]
                packed[r, fl, j] = p
                edges[r] = jnp.where(lane == i, pltpu.roll(p, i + 1, axis=1), edges[r])
                edges[2 + r] = jnp.where(lane == i, pltpu.roll(p, i, axis=1), edges[2 + r])
        return tuple(edges)

    edges = lax.fori_loop(0, FIELDS, pack, tuple(jnp.zeros((8, LANES), F32) for _ in range(4)))
    for n in range(4):
        edge_out[n // 2, n % 2] = edges[n]

    local[2].wait()
    local[3].wait()
    for copy in swaps:
        copy.wait_recv()
    high = (lax.broadcasted_iota(jnp.int32, (1, LANES), 1) & 4) != 0
    for g in range(4):
        first, second = small[0, g], small[1, g]
        both = jnp.where(
            core == 0,
            jnp.where(high, pltpu.roll(second, 4, axis=1), first),
            jnp.where(high, second, pltpu.roll(first, LANES - 4, axis=1)),
        )
        buf[pl.ds(16 * g, 16), 8] = jnp.broadcast_to(both, (16, 1, LANES))

    @pl.when(jnp.logical_not(is_root))
    def _():
        pl.semaphore_wait(go_sem, 1)

    for i in ORDER:
        pf, py = (f + (i >> 2)) & 15, (y + (i & 3)) & 3
        pltpu.make_async_remote_copy(
            src_ref=buf.at[pf * 4 + py], dst_ref=recv.at[chip], send_sem=all_send, recv_sem=all_recv,
            device_id=(pf, py * 2 + core), device_id_type=MESH,
        ).start()
    for pair in zip(halos[0][3:], halos[1][3:]):
        for copy in pair:
            copy.start()
    own = pltpu.make_async_copy(buf.at[chip], recv.at[chip], local_sem.at[4])
    own.start()
    edge_copies = [
        pltpu.make_async_remote_copy(
            src_ref=edge_out.at[n], dst_ref=edge_in.at[n], send_sem=edge_send.at[n], recv_sem=edge_recv.at[n],
            device_id=(f, (c + step) & 7), device_id_type=MESH,
        )
        for n, step in ((0, 1), (1, 7))
    ]
    for copy in edge_copies:
        copy.start()

    local[1].wait()
    t = target[...]
    owner_hot = (lax.broadcasted_iota(jnp.int32, (FACES * COLS, 256), 0) == t).astype(F32)
    before = (
        lax.broadcasted_iota(jnp.int32, (256, 256), 0) < lax.broadcasted_iota(jnp.int32, (256, 256), 1)
    ).astype(F32)
    running = jnp.dot(owner_hot.astype(BF16), before.astype(BF16), preferred_element_type=F32)
    rank = jnp.sum(owner_hot * running, axis=0, keepdims=True)
    row = ((t >> 1) * ROWS + (t & 1) * 4).astype(F32) + rank
    slots = lax.broadcasted_iota(jnp.int32, (CHIPS * ROWS, 256), 0).astype(F32)
    hot[...] = (slots == row).astype(F32).astype(BF16)

    for copy in edge_copies:
        copy.wait_recv()

    def smooth(fl, carry):
        for j in range(STEPS):
            i = fl * STEPS + j
            for r in range(2):
                p = packed[r, fl, j]
                left = jnp.where(lane == 0, pltpu.roll(edge_in[0, r], LANES - i, axis=1), pltpu.roll(p, 1, axis=1))
                right = jnp.where(
                    lane == LANES - 1,
                    pltpu.roll(edge_in[1, r], LANES - 1 - i, axis=1),
                    pltpu.roll(p, LANES - 1, axis=1),
                )
                base[r, fl, j] = SMOOTHING * (packed[1 - r, fl, j] + left + right - 4.0 * p)
        return carry

    lax.fori_loop(0, FIELDS, smooth, 0)

    own.wait()
    pltpu.make_async_copy(recv.at[pl.ds(0, CHIPS - 1)], recv.at[pl.ds(0, CHIPS - 1)], all_recv).wait()
    received = recv.reshape(CHIPS * ROWS, LANES)
    columns = lookup(received[...], hot[...])
    kappa_t[0] = columns[:, :LANES]
    kappa_t[1] = columns[:, LANES:]
    flux_hot = (lax.broadcasted_iota(jnp.int32, (CHIPS, 256), 0) == (t >> 1)).astype(F32)
    flux = lookup(received[pl.ds(8, CHIPS, stride=ROWS), :], flux_hot.astype(BF16))
    wanted = rank + ((t & 1) * 4 + ((f & 3) * 32 + y * 8)).astype(F32)
    lanes_at = lax.broadcasted_iota(jnp.int32, (LANES, 256), 0).astype(F32)
    heat = jnp.sum(jnp.where(lanes_at == wanted, flux, 0.0), axis=0, keepdims=True)
    heat = [jnp.where(sub == BLOCKS - 1, heat[:, r * LANES : (r + 1) * LANES], 0.0) for r in range(2)]

    def interface(j):
        return jnp.stack([kappa_t[r, pl.ds(j, BLOCKS, stride=STEPS), :] for r in range(2)])

    subs = jnp.stack([sub, sub])
    ks = [interface(j) for j in range(STEPS)]
    last = jnp.where(subs == BLOCKS - 1, 0.0, ks[-1])
    above = jnp.where(subs == 0, 0.0, pltpu.roll(ks[-1], 1, axis=1))
    q = 1.0 + above
    u = above
    d = packed[:, :, 0]
    work[:, :, 0] = d
    us, rps, gs = [u], [], []
    for j in range(1, STEPS + 1):
        k = ks[j - 1]
        pivot = q + k
        if j == STEPS:
            break
        rp = 1.0 / pivot
        g = k * rp
        q = 1.0 + (k * q) * rp
        d = packed[:, :, j] + g[:, None] * d
        u = g * u
        if j == STEPS - 1:
            d = jnp.concatenate([(d[:, :1] + jnp.stack(heat)[:, None]), d[:, 1:]], axis=1)
        else:
            work[:, :, j] = d
        us.append(u)
        rps.append(rp)
        gs.append(g)
    v = rps[-1][:, None] * work[:, :, STEPS - 2]
    w = gs[-1]
    u0 = rps[-1] * us[STEPS - 2]
    work[:, :, STEPS - 2] = v
    u_all, w_all = [None] * STEPS, [None] * STEPS
    u_all[STEPS - 2], w_all[STEPS - 2] = u0, w
    for j in range(STEPS - 3, -1, -1):
        v = rps[j][:, None] * work[:, :, j] + gs[j][:, None] * v
        u0 = rps[j] * us[j] + gs[j] * u0
        w = gs[j] * w
        work[:, :, j] = v
        u_all[j], w_all[j] = u0, w

    def prev(value, n=1):
        return pltpu.roll(value, n, axis=value.ndim - 2)

    def following(value, n=1):
        return pltpu.roll(value, BLOCKS - n, axis=value.ndim - 2)

    inverse = 1.0 / (pivot - last * following(u0))
    a = us[STEPS - 1] * inverse
    b = last * following(w) * inverse
    rhs = (d + last[:, None] * following(v)) * inverse[:, None]
    for n in (1, 2, 4):
        inverse = 1.0 / (1.0 - a * prev(b, n) - b * following(a, n))
        rhs = (rhs + a[:, None] * prev(rhs, n) + b[:, None] * following(rhs, n)) * inverse[:, None]
        a, b = a * prev(a, n) * inverse, b * following(b, n) * inverse
    bottom = rhs
    top = jnp.where(subs[:, None] == 0, 0.0, prev(bottom))
    for j in range(STEPS - 1):
        base[:, :, j] += work[:, :, j] + u_all[j][:, None] * top + w_all[j][:, None] * bottom
    base[:, :, STEPS - 1] += bottom

    halo_rows = halo.reshape(2 * FIELDS * LEVELS, LANES)
    out_rows = out.reshape(FIELDS * LEVELS * 2, LANES)
    for fl in range(FIELDS):
        for d_at in range(2):
            halos[d_at][fl].wait_recv()
        for j in range(STEPS):
            for r in range(2):
                beside = halo_rows[pl.ds((r * FIELDS + fl) * LEVELS + j, BLOCKS, stride=STEPS), :]
                out_rows[pl.ds(fl * 2 * LEVELS + 2 * j + r, BLOCKS, stride=2 * STEPS), :] = (
                    base[r, fl, j] + SMOOTHING * beside
                )
    pltpu.make_async_copy(recv.at[pl.ds(0, CHIPS - 1)], recv.at[pl.ds(0, CHIPS - 1)], all_send).wait()
    for copy in swaps + edge_copies + halos[0] + halos[1]:
        copy.wait_send()


def shards(prognostic, diffusivity, surface_flux, assignment):
    x = prognostic.reshape(FIELDS * LEVELS, 2, 1, LANES)
    k = diffusivity.reshape(CHIPS, 2, 4, 1, LEVELS)
    flux = surface_flux.reshape(4, 1, LANES)
    target = assignment.reshape(1, 256)
    any_spec = pl.BlockSpec(memory_space=pl.ANY)
    dma = pltpu.SemaphoreType.DMA
    wide = (2, FIELDS, STEPS, BLOCKS, LANES)
    result = pl.pallas_call(
        kernel,
        out_shape=pltpu.VMEM(x.shape, F32),
        name="exchange",
        in_specs=[any_spec] * 4,
        out_specs=pl.BlockSpec(memory_space=pltpu.VMEM),
        scratch_shapes=[
            pltpu.VMEM(x.shape, F32),
            pltpu.VMEM((1, 256), jnp.int32),
            pltpu.VMEM((2, 4, 1, LANES), F32),
            pltpu.VMEM((CHIPS, ROWS, 1, LANES), F32),
            pltpu.VMEM((CHIPS, ROWS, 1, LANES), F32),
            pltpu.VMEM((2, FIELDS * LEVELS, 1, LANES), F32),
            pltpu.VMEM(wide, F32),
            pltpu.VMEM(wide, F32),
            pltpu.VMEM(wide, F32),
            pltpu.VMEM((2, 2, BLOCKS, LANES), F32),
            pltpu.VMEM((2, 2, BLOCKS, LANES), F32),
            pltpu.VMEM((CHIPS * ROWS, 256), BF16),
            pltpu.VMEM((2, LEVELS, LANES), F32),
            dma((5,)),
            dma((2,)),
            dma((2,)),
            dma((2, FIELDS)),
            dma((2, FIELDS)),
            dma((2,)),
            dma((2,)),
            dma,
            dma,
            pltpu.SemaphoreType.REGULAR,
            pltpu.SemaphoreType.REGULAR,
            pltpu.SemaphoreType.REGULAR,
        ],
        compiler_params=pltpu.CompilerParams(
            collective_id=0, has_side_effects=True, vmem_limit_bytes=56 << 20
        ),
    )(x, k, flux, target)
    return result.reshape(prognostic.shape)


def solution(mesh):
    return jax.shard_map(
        shards,
        mesh=mesh,
        in_specs=(
            P(None, None, "face", "col"),
            P("face", "col", None, None),
            P("face", "col", None),
            P("face", "col", None, None),
        ),
        out_specs=P(None, None, "face", "col"),
        check_vma=False,
    )
```

```python
import functools

import jax
import jax.numpy as jnp
from jax import lax
from jax.experimental import pallas as pl
from jax.experimental.pallas import tpu as pltpu
from jax.sharding import PartitionSpec as P

MESH = pl.DeviceIdType.MESH
SMOOTHING = 0.2
FACES, COLS = 16, 8
CHIPS = 64
FIELDS, LEVELS, LANES = 5, 128, 128
BLOCKS, STEPS = 8, 16
ROWS = 9
AHEAD = 2
F32, BF16 = jnp.float32, jnp.bfloat16


def split2(value):
    high = value.astype(BF16)
    return high, (value - high.astype(F32)).astype(BF16)


def lookup(table, hot):
    dims = (((0,), (0,)), ((), ()))
    high, low = split2(table)
    return lax.dot_general(high, hot, dims, preferred_element_type=F32) + lax.dot_general(
        low, hot, dims, preferred_element_type=F32
    )


def kernel(
    x_hbm, k_hbm, flux_hbm, assign_hbm, out,
    xin, target, small, buf, recv, halo, packed, base, work, edge_out, edge_in, hot, kappa_t,
    local_sem, swap_send, swap_recv, halo_send, halo_recv, edge_send, edge_recv, all_send, all_recv,
    go_sem, near_sem,
):
    f, c = lax.axis_index("face"), lax.axis_index("col")
    y, core = c >> 1, c & 1
    chip = f * 4 + y
    up, down = (f + 1) & 15, (f + 15) & 15
    partner = (f, c ^ 1)

    barrier = pltpu.get_barrier_semaphore()
    first, second = y << 1, (y << 1) | 1
    for i in range(1, FACES):
        pl.semaphore_signal(barrier, inc=1, device_id=((f + i) & 15, second), device_id_type=MESH)
    y_peers = [(f, (((y + i) & 3) << 1) | 1) for i in range(1, 4)]
    for peer in y_peers + [(up, first), (down, first), partner]:
        pl.semaphore_signal(barrier, inc=1, device_id=peer, device_id_type=MESH)

    local = [
        pltpu.make_async_copy(x_hbm, xin, local_sem.at[0]),
        pltpu.make_async_copy(assign_hbm, target, local_sem.at[1]),
        pltpu.make_async_copy(k_hbm.at[:, core], buf.at[:, pl.ds(4 * core, 4)], local_sem.at[2]),
        pltpu.make_async_copy(flux_hbm, small.at[core], local_sem.at[3]),
    ]
    for copy in local:
        copy.start()

    swaps = [
        pltpu.make_async_remote_copy(
            src_ref=src, dst_ref=dst, send_sem=swap_send.at[i], recv_sem=swap_recv.at[i],
            device_id=partner, device_id_type=MESH,
        )
        for i, (src, dst) in enumerate((
            (k_hbm.at[:, 1 - core], buf.at[:, pl.ds(4 * core, 4)]),
            (flux_hbm, small.at[core]),
        ))
    ]
    halos = [
        [
            pltpu.make_async_remote_copy(
                src_ref=x_hbm.at[pl.ds(fl * LEVELS, LEVELS), row], dst_ref=halo.at[d, pl.ds(fl * LEVELS, LEVELS)],
                send_sem=halo_send.at[d, fl], recv_sem=halo_recv.at[d, fl],
                device_id=(peer, c), device_id_type=MESH,
            )
            for fl in range(FIELDS)
        ]
        for d, row, peer in ((0, 1, up), (1, 0, down))
    ]

    @pl.when(core == 0)
    def _():
        pl.semaphore_wait(barrier, 5)
        pl.semaphore_signal(near_sem, inc=1, device_id=partner, device_id_type=MESH)

    @pl.when(core == 1)
    def _():
        pl.semaphore_wait(near_sem, 1)

    for pair in zip(halos[0][:AHEAD], halos[1][:AHEAD]):
        for copy in pair:
            copy.start()
    for copy in swaps:
        copy.start()

    @pl.when(core == 1)
    def _():
        pl.semaphore_wait(barrier, 2 * (FACES - 1 + 3) + 1)
        for peer in y_peers:
            pl.semaphore_signal(go_sem, inc=1, device_id=peer, device_id_type=MESH)

    lane = lax.broadcasted_iota(jnp.int32, (8, LANES), 1)
    sub = lax.broadcasted_iota(jnp.int32, (8, LANES), 0)
    local[0].wait()
    x_rows = xin.reshape(FIELDS * LEVELS * 2, LANES)

    def pack(fl, edges):
        edges = list(edges)
        for j in range(STEPS):
            i = fl * STEPS + j
            for r in range(2):
                p = x_rows[pl.ds(fl * 2 * LEVELS + 2 * j + r, BLOCKS, stride=2 * STEPS), :]
                packed[r, fl, j] = p
                edges[r] = jnp.where(lane == i, pltpu.roll(p, i + 1, axis=1), edges[r])
                edges[2 + r] = jnp.where(lane == i, pltpu.roll(p, i, axis=1), edges[2 + r])
        return tuple(edges)

    edges = lax.fori_loop(0, FIELDS, pack, tuple(jnp.zeros((8, LANES), F32) for _ in range(4)))
    for n in range(4):
        edge_out[n // 2, n % 2] = edges[n]

    local[2].wait()
    local[3].wait()
    for copy in swaps:
        copy.wait_recv()
    high = (lax.broadcasted_iota(jnp.int32, (1, LANES), 1) & 4) != 0
    for g in range(4):
        first, second = small[0, g], small[1, g]
        both = jnp.where(
            core == 0,
            jnp.where(high, pltpu.roll(second, 4, axis=1), first),
            jnp.where(high, second, pltpu.roll(first, LANES - 4, axis=1)),
        )
        buf[pl.ds(16 * g, 16), 8] = jnp.broadcast_to(both, (16, 1, LANES))

    def send(pf, py):
        pltpu.make_async_remote_copy(
            src_ref=buf.at[pf * 4 + py], dst_ref=recv.at[chip], send_sem=all_send, recv_sem=all_recv,
            device_id=(pf, py * 2 + core), device_id_type=MESH,
        ).start()

    @pl.when(core == 1)
    def _():
        pl.semaphore_wait(go_sem, len(y_peers))
        pl.semaphore_signal(near_sem, inc=1, device_id=partner, device_id_type=MESH)

    @pl.when(core == 0)
    def _():
        pl.semaphore_wait(near_sem, 1)

    for i in range(1, CHIPS):
        send((f + (i >> 2)) & 15, (y + (i & 3)) & 3)
    for pair in zip(halos[0][AHEAD:], halos[1][AHEAD:]):
        for copy in pair:
            copy.start()
    own = pltpu.make_async_copy(buf.at[chip], recv.at[chip], local_sem.at[4])
    own.start()
    edge_copies = [
        pltpu.make_async_remote_copy(
            src_ref=edge_out.at[n], dst_ref=edge_in.at[n], send_sem=edge_send.at[n], recv_sem=edge_recv.at[n],
            device_id=(f, (c + step) & 7), device_id_type=MESH,
        )
        for n, step in ((0, 1), (1, 7))
    ]
    for copy in edge_copies:
        copy.start()

    local[1].wait()
    t = target[...]
    owner_hot = (lax.broadcasted_iota(jnp.int32, (FACES * COLS, 256), 0) == t).astype(F32)
    before = (
        lax.broadcasted_iota(jnp.int32, (256, 256), 0) < lax.broadcasted_iota(jnp.int32, (256, 256), 1)
    ).astype(F32)
    running = jnp.dot(owner_hot.astype(BF16), before.astype(BF16), preferred_element_type=F32)
    rank = jnp.sum(owner_hot * running, axis=0, keepdims=True)
    row = ((t >> 1) * ROWS + (t & 1) * 4).astype(F32) + rank
    slots = lax.broadcasted_iota(jnp.int32, (CHIPS * ROWS, 256), 0).astype(F32)
    hot[...] = (slots == row).astype(F32).astype(BF16)

    for copy in edge_copies:
        copy.wait_recv()

    def smooth(fl, carry):
        for j in range(STEPS):
            i = fl * STEPS + j
            for r in range(2):
                p = packed[r, fl, j]
                left = jnp.where(lane == 0, pltpu.roll(edge_in[0, r], LANES - i, axis=1), pltpu.roll(p, 1, axis=1))
                right = jnp.where(
                    lane == LANES - 1,
                    pltpu.roll(edge_in[1, r], LANES - 1 - i, axis=1),
                    pltpu.roll(p, LANES - 1, axis=1),
                )
                base[r, fl, j] = SMOOTHING * (packed[1 - r, fl, j] + left + right - 4.0 * p)
        return carry

    lax.fori_loop(0, FIELDS, smooth, 0)

    own.wait()
    pltpu.make_async_copy(recv.at[pl.ds(0, CHIPS - 1)], recv.at[pl.ds(0, CHIPS - 1)], all_recv).wait()
    received = recv.reshape(CHIPS * ROWS, LANES)
    columns = lookup(received[...], hot[...])
    kappa_t[0] = columns[:, :LANES]
    kappa_t[1] = columns[:, LANES:]
    flux_hot = (lax.broadcasted_iota(jnp.int32, (CHIPS, 256), 0) == (t >> 1)).astype(F32)
    flux = lookup(received[pl.ds(8, CHIPS, stride=ROWS), :], flux_hot.astype(BF16))
    wanted = rank + ((t & 1) * 4 + ((f & 3) * 32 + y * 8)).astype(F32)
    lanes_at = lax.broadcasted_iota(jnp.int32, (LANES, 256), 0).astype(F32)
    heat = jnp.sum(jnp.where(lanes_at == wanted, flux, 0.0), axis=0, keepdims=True)
    heat = [jnp.where(sub == BLOCKS - 1, heat[:, r * LANES : (r + 1) * LANES], 0.0) for r in range(2)]

    def interface(j):
        return jnp.stack([kappa_t[r, pl.ds(j, BLOCKS, stride=STEPS), :] for r in range(2)])

    subs = jnp.stack([sub, sub])
    ks = [interface(j) for j in range(STEPS)]
    last = jnp.where(subs == BLOCKS - 1, 0.0, ks[-1])
    above = jnp.where(subs == 0, 0.0, pltpu.roll(ks[-1], 1, axis=1))
    q = 1.0 + above
    u = above
    d = packed[:, :, 0]
    work[:, :, 0] = d
    us, rps, gs = [u], [], []
    for j in range(1, STEPS + 1):
        k = ks[j - 1]
        pivot = q + k
        if j == STEPS:
            break
        rp = 1.0 / pivot
        g = k * rp
        q = 1.0 + (k * q) * rp
        d = packed[:, :, j] + g[:, None] * d
        u = g * u
        if j == STEPS - 1:
            d = jnp.concatenate([(d[:, :1] + jnp.stack(heat)[:, None]), d[:, 1:]], axis=1)
        else:
            work[:, :, j] = d
        us.append(u)
        rps.append(rp)
        gs.append(g)
    v = rps[-1][:, None] * work[:, :, STEPS - 2]
    w = gs[-1]
    u0 = rps[-1] * us[STEPS - 2]
    work[:, :, STEPS - 2] = v
    u_all, w_all = [None] * STEPS, [None] * STEPS
    u_all[STEPS - 2], w_all[STEPS - 2] = u0, w
    for j in range(STEPS - 3, -1, -1):
        v = rps[j][:, None] * work[:, :, j] + gs[j][:, None] * v
        u0 = rps[j] * us[j] + gs[j] * u0
        w = gs[j] * w
        work[:, :, j] = v
        u_all[j], w_all[j] = u0, w

    def prev(value, n=1):
        return pltpu.roll(value, n, axis=value.ndim - 2)

    def following(value, n=1):
        return pltpu.roll(value, BLOCKS - n, axis=value.ndim - 2)

    inverse = 1.0 / (pivot - last * following(u0))
    a = us[STEPS - 1] * inverse
    b = last * following(w) * inverse
    rhs = (d + last[:, None] * following(v)) * inverse[:, None]
    for n in (1, 2, 4):
        inverse = 1.0 / (1.0 - a * prev(b, n) - b * following(a, n))
        rhs = (rhs + a[:, None] * prev(rhs, n) + b[:, None] * following(rhs, n)) * inverse[:, None]
        a, b = a * prev(a, n) * inverse, b * following(b, n) * inverse
    bottom = rhs
    top = jnp.where(subs[:, None] == 0, 0.0, prev(bottom))
    for j in range(STEPS - 1):
        base[:, :, j] += work[:, :, j] + u_all[j][:, None] * top + w_all[j][:, None] * bottom
    base[:, :, STEPS - 1] += bottom

    halo_rows = halo.reshape(2 * FIELDS * LEVELS, LANES)
    out_rows = out.reshape(FIELDS * LEVELS * 2, LANES)
    for fl in range(FIELDS):
        for d_at in range(2):
            halos[d_at][fl].wait_recv()
        for j in range(STEPS):
            for r in range(2):
                beside = halo_rows[pl.ds((r * FIELDS + fl) * LEVELS + j, BLOCKS, stride=STEPS), :]
                out_rows[pl.ds(fl * 2 * LEVELS + 2 * j + r, BLOCKS, stride=2 * STEPS), :] = (
                    base[r, fl, j] + SMOOTHING * beside
                )
    pltpu.make_async_copy(recv.at[pl.ds(0, CHIPS - 1)], recv.at[pl.ds(0, CHIPS - 1)], all_send).wait()
    for copy in swaps + edge_copies + halos[0] + halos[1]:
        copy.wait_send()


def shards(prognostic, diffusivity, surface_flux, assignment):
    x = prognostic.reshape(FIELDS * LEVELS, 2, 1, LANES)
    k = diffusivity.reshape(CHIPS, 2, 4, 1, LEVELS)
    flux = surface_flux.reshape(4, 1, LANES)
    target = assignment.reshape(1, 256)
    any_spec = pl.BlockSpec(memory_space=pl.ANY)
    dma = pltpu.SemaphoreType.DMA
    wide = (2, FIELDS, STEPS, BLOCKS, LANES)
    result = pl.pallas_call(
        kernel,
        out_shape=pltpu.VMEM(x.shape, F32),
        name="exchange",
        in_specs=[any_spec] * 4,
        out_specs=pl.BlockSpec(memory_space=pltpu.VMEM),
        scratch_shapes=[
            pltpu.VMEM(x.shape, F32),
            pltpu.VMEM((1, 256), jnp.int32),
            pltpu.VMEM((2, 4, 1, LANES), F32),
            pltpu.VMEM((CHIPS, ROWS, 1, LANES), F32),
            pltpu.VMEM((CHIPS, ROWS, 1, LANES), F32),
            pltpu.VMEM((2, FIELDS * LEVELS, 1, LANES), F32),
            pltpu.VMEM(wide, F32),
            pltpu.VMEM(wide, F32),
            pltpu.VMEM(wide, F32),
            pltpu.VMEM((2, 2, BLOCKS, LANES), F32),
            pltpu.VMEM((2, 2, BLOCKS, LANES), F32),
            pltpu.VMEM((CHIPS * ROWS, 256), BF16),
            pltpu.VMEM((2, LEVELS, LANES), F32),
            dma((5,)),
            dma((2,)),
            dma((2,)),
            dma((2, FIELDS)),
            dma((2, FIELDS)),
            dma((2,)),
            dma((2,)),
            dma,
            dma,
            pltpu.SemaphoreType.REGULAR,
            pltpu.SemaphoreType.REGULAR,
        ],
        compiler_params=pltpu.CompilerParams(
            collective_id=0, has_side_effects=True, vmem_limit_bytes=56 << 20
        ),
    )(x, k, flux, target)
    return result.reshape(prognostic.shape)


def solution(mesh):
    return jax.shard_map(
        shards,
        mesh=mesh,
        in_specs=(
            P(None, None, "face", "col"),
            P("face", "col", None, None),
            P("face", "col", None),
            P("face", "col", None, None),
        ),
        out_specs=P(None, None, "face", "col"),
        check_vma=False,
    )
```

```python
import functools

import jax
import jax.numpy as jnp
from jax import lax
from jax.experimental import pallas as pl
from jax.experimental.pallas import tpu as pltpu
from jax.sharding import PartitionSpec as P

MESH = pl.DeviceIdType.MESH
SMOOTHING = 0.2
FACES, COLS = 16, 8
CHIPS = 64
FIELDS, LEVELS, LANES = 5, 128, 128
BLOCKS, STEPS = 8, 16
ROWS = 9
AHEAD = 2
F32, BF16 = jnp.float32, jnp.bfloat16


def split2(value):
    high = value.astype(BF16)
    return high, (value - high.astype(F32)).astype(BF16)


def lookup(table, hot):
    dims = (((0,), (0,)), ((), ()))
    high, low = split2(table)
    return lax.dot_general(high, hot, dims, preferred_element_type=F32) + lax.dot_general(
        low, hot, dims, preferred_element_type=F32
    )


def kernel(
    x_hbm, k_hbm, flux_hbm, assign_hbm, out,
    xin, target, small, buf, recv, halo, packed, base, work, edge_out, edge_in, hot, kappa_t,
    local_sem, swap_send, swap_recv, halo_send, halo_recv, edge_send, edge_recv, all_send, all_recv,
    go_sem, near_sem,
):
    f, c = lax.axis_index("face"), lax.axis_index("col")
    y, core = c >> 1, c & 1
    chip = f * 4 + y
    up, down = (f + 1) & 15, (f + 15) & 15
    partner = (f, c ^ 1)

    barrier = pltpu.get_barrier_semaphore()
    first, second = y << 1, (y << 1) | 1
    for i in range(1, FACES):
        pl.semaphore_signal(barrier, inc=1, device_id=((f + i) & 15, second), device_id_type=MESH)
    y_peers = [(f, (((y + i) & 3) << 1) | 1) for i in range(1, 4)]
    for peer in y_peers + [(up, first), (down, first), partner]:
        pl.semaphore_signal(barrier, inc=1, device_id=peer, device_id_type=MESH)

    local = [
        pltpu.make_async_copy(x_hbm, xin, local_sem.at[0]),
        pltpu.make_async_copy(assign_hbm, target, local_sem.at[1]),
        pltpu.make_async_copy(k_hbm.at[:, core], buf.at[:, pl.ds(4 * core, 4)], local_sem.at[2]),
        pltpu.make_async_copy(flux_hbm, small.at[core], local_sem.at[3]),
    ]
    for copy in local:
        copy.start()

    swaps = [
        pltpu.make_async_remote_copy(
            src_ref=src, dst_ref=dst, send_sem=swap_send.at[i], recv_sem=swap_recv.at[i],
            device_id=partner, device_id_type=MESH,
        )
        for i, (src, dst) in enumerate((
            (k_hbm.at[:, 1 - core], buf.at[:, pl.ds(4 * core, 4)]),
            (flux_hbm, small.at[core]),
        ))
    ]
    halos = [
        [
            pltpu.make_async_remote_copy(
                src_ref=x_hbm.at[pl.ds(fl * LEVELS, LEVELS), row], dst_ref=halo.at[d, pl.ds(fl * LEVELS, LEVELS)],
                send_sem=halo_send.at[d, fl], recv_sem=halo_recv.at[d, fl],
                device_id=(peer, c), device_id_type=MESH,
            )
            for fl in range(FIELDS)
        ]
        for d, row, peer in ((0, 1, up), (1, 0, down))
    ]

    @pl.when(core == 0)
    def _():
        pl.semaphore_wait(barrier, 5)
        pl.semaphore_signal(near_sem, inc=1, device_id=partner, device_id_type=MESH)

    @pl.when(core == 1)
    def _():
        pl.semaphore_wait(near_sem, 1)

    for pair in zip(halos[0][:AHEAD], halos[1][:AHEAD]):
        for copy in pair:
            copy.start()
    for copy in swaps:
        copy.start()

    @pl.when(y < 2)
    def _():
        for n in range(2):
            halos[n][2].start()

    @pl.when(core == 1)
    def _():
        pl.semaphore_wait(barrier, 2 * (FACES - 1 + 3) + 1)
        for peer in y_peers:
            pl.semaphore_signal(go_sem, inc=1, device_id=peer, device_id_type=MESH)

    lane = lax.broadcasted_iota(jnp.int32, (8, LANES), 1)
    sub = lax.broadcasted_iota(jnp.int32, (8, LANES), 0)
    local[0].wait()
    x_rows = xin.reshape(FIELDS * LEVELS * 2, LANES)

    def pack(fl, edges):
        edges = list(edges)
        for j in range(STEPS):
            i = fl * STEPS + j
            for r in range(2):
                p = x_rows[pl.ds(fl * 2 * LEVELS + 2 * j + r, BLOCKS, stride=2 * STEPS), :]
                packed[r, fl, j] = p
                edges[r] = jnp.where(lane == i, pltpu.roll(p, i + 1, axis=1), edges[r])
                edges[2 + r] = jnp.where(lane == i, pltpu.roll(p, i, axis=1), edges[2 + r])
        return tuple(edges)

    edges = lax.fori_loop(0, FIELDS, pack, tuple(jnp.zeros((8, LANES), F32) for _ in range(4)))
    for n in range(4):
        edge_out[n // 2, n % 2] = edges[n]

    local[2].wait()
    local[3].wait()
    for copy in swaps:
        copy.wait_recv()
    high = (lax.broadcasted_iota(jnp.int32, (1, LANES), 1) & 4) != 0
    for g in range(4):
        first, second = small[0, g], small[1, g]
        both = jnp.where(
            core == 0,
            jnp.where(high, pltpu.roll(second, 4, axis=1), first),
            jnp.where(high, second, pltpu.roll(first, LANES - 4, axis=1)),
        )
        buf[pl.ds(16 * g, 16), 8] = jnp.broadcast_to(both, (16, 1, LANES))

    def send(pf, py):
        pltpu.make_async_remote_copy(
            src_ref=buf.at[pf * 4 + py], dst_ref=recv.at[chip], send_sem=all_send, recv_sem=all_recv,
            device_id=(pf, py * 2 + core), device_id_type=MESH,
        ).start()

    @pl.when(core == 1)
    def _():
        pl.semaphore_wait(go_sem, len(y_peers))
        pl.semaphore_signal(near_sem, inc=1, device_id=partner, device_id_type=MESH)

    @pl.when(core == 0)
    def _():
        pl.semaphore_wait(near_sem, 1)

    for i in range(1, CHIPS):
        send((f + (i >> 2)) & 15, (y + (i & 3)) & 3)

    @pl.when(jnp.logical_not(y < 2))
    def _():
        for n in range(2):
            halos[n][2].start()

    for pair in zip(halos[0][AHEAD + 1:], halos[1][AHEAD + 1:]):
        for copy in pair:
            copy.start()
    own = pltpu.make_async_copy(buf.at[chip], recv.at[chip], local_sem.at[4])
    own.start()
    edge_copies = [
        pltpu.make_async_remote_copy(
            src_ref=edge_out.at[n], dst_ref=edge_in.at[n], send_sem=edge_send.at[n], recv_sem=edge_recv.at[n],
            device_id=(f, (c + step) & 7), device_id_type=MESH,
        )
        for n, step in ((0, 1), (1, 7))
    ]
    for copy in edge_copies:
        copy.start()

    local[1].wait()
    t = target[...]
    owner_hot = (lax.broadcasted_iota(jnp.int32, (FACES * COLS, 256), 0) == t).astype(F32)
    before = (
        lax.broadcasted_iota(jnp.int32, (256, 256), 0) < lax.broadcasted_iota(jnp.int32, (256, 256), 1)
    ).astype(F32)
    running = jnp.dot(owner_hot.astype(BF16), before.astype(BF16), preferred_element_type=F32)
    rank = jnp.sum(owner_hot * running, axis=0, keepdims=True)
    row = ((t >> 1) * ROWS + (t & 1) * 4).astype(F32) + rank
    slots = lax.broadcasted_iota(jnp.int32, (CHIPS * ROWS, 256), 0).astype(F32)
    hot[...] = (slots == row).astype(F32).astype(BF16)

    for copy in edge_copies:
        copy.wait_recv()

    def smooth(fl, carry):
        for j in range(STEPS):
            i = fl * STEPS + j
            for r in range(2):
                p = packed[r, fl, j]
                left = jnp.where(lane == 0, pltpu.roll(edge_in[0, r], LANES - i, axis=1), pltpu.roll(p, 1, axis=1))
                right = jnp.where(
                    lane == LANES - 1,
                    pltpu.roll(edge_in[1, r], LANES - 1 - i, axis=1),
                    pltpu.roll(p, LANES - 1, axis=1),
                )
                base[r, fl, j] = SMOOTHING * (packed[1 - r, fl, j] + left + right - 4.0 * p)
        return carry

    lax.fori_loop(0, FIELDS, smooth, 0)

    own.wait()
    pltpu.make_async_copy(recv.at[pl.ds(0, CHIPS - 1)], recv.at[pl.ds(0, CHIPS - 1)], all_recv).wait()
    received = recv.reshape(CHIPS * ROWS, LANES)
    columns = lookup(received[...], hot[...])
    kappa_t[0] = columns[:, :LANES]
    kappa_t[1] = columns[:, LANES:]
    flux_hot = (lax.broadcasted_iota(jnp.int32, (CHIPS, 256), 0) == (t >> 1)).astype(F32)
    flux = lookup(received[pl.ds(8, CHIPS, stride=ROWS), :], flux_hot.astype(BF16))
    wanted = rank + ((t & 1) * 4 + ((f & 3) * 32 + y * 8)).astype(F32)
    lanes_at = lax.broadcasted_iota(jnp.int32, (LANES, 256), 0).astype(F32)
    heat = jnp.sum(jnp.where(lanes_at == wanted, flux, 0.0), axis=0, keepdims=True)
    heat = [jnp.where(sub == BLOCKS - 1, heat[:, r * LANES : (r + 1) * LANES], 0.0) for r in range(2)]

    def interface(j):
        return jnp.stack([kappa_t[r, pl.ds(j, BLOCKS, stride=STEPS), :] for r in range(2)])

    subs = jnp.stack([sub, sub])
    ks = [interface(j) for j in range(STEPS)]
    last = jnp.where(subs == BLOCKS - 1, 0.0, ks[-1])
    above = jnp.where(subs == 0, 0.0, pltpu.roll(ks[-1], 1, axis=1))
    q = 1.0 + above
    u = above
    d = packed[:, :, 0]
    work[:, :, 0] = d
    us, rps, gs = [u], [], []
    for j in range(1, STEPS + 1):
        k = ks[j - 1]
        pivot = q + k
        if j == STEPS:
            break
        rp = 1.0 / pivot
        g = k * rp
        q = 1.0 + (k * q) * rp
        d = packed[:, :, j] + g[:, None] * d
        u = g * u
        if j == STEPS - 1:
            d = jnp.concatenate([(d[:, :1] + jnp.stack(heat)[:, None]), d[:, 1:]], axis=1)
        else:
            work[:, :, j] = d
        us.append(u)
        rps.append(rp)
        gs.append(g)
    v = rps[-1][:, None] * work[:, :, STEPS - 2]
    w = gs[-1]
    u0 = rps[-1] * us[STEPS - 2]
    work[:, :, STEPS - 2] = v
    u_all, w_all = [None] * STEPS, [None] * STEPS
    u_all[STEPS - 2], w_all[STEPS - 2] = u0, w
    for j in range(STEPS - 3, -1, -1):
        v = rps[j][:, None] * work[:, :, j] + gs[j][:, None] * v
        u0 = rps[j] * us[j] + gs[j] * u0
        w = gs[j] * w
        work[:, :, j] = v
        u_all[j], w_all[j] = u0, w

    def prev(value, n=1):
        return pltpu.roll(value, n, axis=value.ndim - 2)

    def following(value, n=1):
        return pltpu.roll(value, BLOCKS - n, axis=value.ndim - 2)

    inverse = 1.0 / (pivot - last * following(u0))
    a = us[STEPS - 1] * inverse
    b = last * following(w) * inverse
    rhs = (d + last[:, None] * following(v)) * inverse[:, None]
    for n in (1, 2, 4):
        inverse = 1.0 / (1.0 - a * prev(b, n) - b * following(a, n))
        rhs = (rhs + a[:, None] * prev(rhs, n) + b[:, None] * following(rhs, n)) * inverse[:, None]
        a, b = a * prev(a, n) * inverse, b * following(b, n) * inverse
    bottom = rhs
    top = jnp.where(subs[:, None] == 0, 0.0, prev(bottom))
    for j in range(STEPS - 1):
        base[:, :, j] += work[:, :, j] + u_all[j][:, None] * top + w_all[j][:, None] * bottom
    base[:, :, STEPS - 1] += bottom

    halo_rows = halo.reshape(2 * FIELDS * LEVELS, LANES)
    out_rows = out.reshape(FIELDS * LEVELS * 2, LANES)
    for fl in range(FIELDS):
        for d_at in range(2):
            halos[d_at][fl].wait_recv()
        for j in range(STEPS):
            for r in range(2):
                beside = halo_rows[pl.ds((r * FIELDS + fl) * LEVELS + j, BLOCKS, stride=STEPS), :]
                out_rows[pl.ds(fl * 2 * LEVELS + 2 * j + r, BLOCKS, stride=2 * STEPS), :] = (
                    base[r, fl, j] + SMOOTHING * beside
                )
    pltpu.make_async_copy(recv.at[pl.ds(0, CHIPS - 1)], recv.at[pl.ds(0, CHIPS - 1)], all_send).wait()
    for copy in swaps + edge_copies + halos[0] + halos[1]:
        copy.wait_send()


def shards(prognostic, diffusivity, surface_flux, assignment):
    x = prognostic.reshape(FIELDS * LEVELS, 2, 1, LANES)
    k = diffusivity.reshape(CHIPS, 2, 4, 1, LEVELS)
    flux = surface_flux.reshape(4, 1, LANES)
    target = assignment.reshape(1, 256)
    any_spec = pl.BlockSpec(memory_space=pl.ANY)
    dma = pltpu.SemaphoreType.DMA
    wide = (2, FIELDS, STEPS, BLOCKS, LANES)
    result = pl.pallas_call(
        kernel,
        out_shape=pltpu.VMEM(x.shape, F32),
        name="exchange",
        in_specs=[any_spec] * 4,
        out_specs=pl.BlockSpec(memory_space=pltpu.VMEM),
        scratch_shapes=[
            pltpu.VMEM(x.shape, F32),
            pltpu.VMEM((1, 256), jnp.int32),
            pltpu.VMEM((2, 4, 1, LANES), F32),
            pltpu.VMEM((CHIPS, ROWS, 1, LANES), F32),
            pltpu.VMEM((CHIPS, ROWS, 1, LANES), F32),
            pltpu.VMEM((2, FIELDS * LEVELS, 1, LANES), F32),
            pltpu.VMEM(wide, F32),
            pltpu.VMEM(wide, F32),
            pltpu.VMEM(wide, F32),
            pltpu.VMEM((2, 2, BLOCKS, LANES), F32),
            pltpu.VMEM((2, 2, BLOCKS, LANES), F32),
            pltpu.VMEM((CHIPS * ROWS, 256), BF16),
            pltpu.VMEM((2, LEVELS, LANES), F32),
            dma((5,)),
            dma((2,)),
            dma((2,)),
            dma((2, FIELDS)),
            dma((2, FIELDS)),
            dma((2,)),
            dma((2,)),
            dma,
            dma,
            pltpu.SemaphoreType.REGULAR,
            pltpu.SemaphoreType.REGULAR,
        ],
        compiler_params=pltpu.CompilerParams(
            collective_id=0, has_side_effects=True, vmem_limit_bytes=56 << 20
        ),
    )(x, k, flux, target)
    return result.reshape(prognostic.shape)


def solution(mesh):
    return jax.shard_map(
        shards,
        mesh=mesh,
        in_specs=(
            P(None, None, "face", "col"),
            P("face", "col", None, None),
            P("face", "col", None),
            P("face", "col", None, None),
        ),
        out_specs=P(None, None, "face", "col"),
        check_vma=False,
    )
```

```python
import functools

import jax
import jax.numpy as jnp
from jax import lax
from jax.experimental import pallas as pl
from jax.experimental.pallas import tpu as pltpu
from jax.sharding import PartitionSpec as P

MESH = pl.DeviceIdType.MESH
SMOOTHING = 0.2
FACES, COLS = 16, 8
CHIPS = 64
FIELDS, LEVELS, LANES = 5, 128, 128
BLOCKS, STEPS = 8, 16
ROWS = 9
AHEAD = 2
F32, BF16 = jnp.float32, jnp.bfloat16


def split2(value):
    high = value.astype(BF16)
    return high, (value - high.astype(F32)).astype(BF16)


def lookup(table, hot):
    dims = (((0,), (0,)), ((), ()))
    high, low = split2(table)
    return lax.dot_general(high, hot, dims, preferred_element_type=F32) + lax.dot_general(
        low, hot, dims, preferred_element_type=F32
    )


def kernel(
    x_hbm, k_hbm, flux_hbm, assign_hbm, out,
    xin, target, small, buf, recv, halo, packed, base, work, edge_out, edge_in, hot, kappa_t,
    local_sem, swap_send, swap_recv, halo_send, halo_recv, edge_send, edge_recv, all_send, all_recv,
    go_sem, near_sem,
):
    f, c = lax.axis_index("face"), lax.axis_index("col")
    y, core = c >> 1, c & 1
    chip = f * 4 + y
    up, down = (f + 1) & 15, (f + 15) & 15
    partner = (f, c ^ 1)

    barrier = pltpu.get_barrier_semaphore()
    first, second = y << 1, (y << 1) | 1
    for i in range(1, FACES):
        pl.semaphore_signal(barrier, inc=1, device_id=((f + i) & 15, second), device_id_type=MESH)
    y_peers = [(f, (((y + i) & 3) << 1) | 1) for i in range(1, 4)]
    for peer in y_peers + [(up, first), (down, first), partner]:
        pl.semaphore_signal(barrier, inc=1, device_id=peer, device_id_type=MESH)

    local = [
        pltpu.make_async_copy(x_hbm, xin, local_sem.at[0]),
        pltpu.make_async_copy(assign_hbm, target, local_sem.at[1]),
        pltpu.make_async_copy(k_hbm.at[:, core], buf.at[:, pl.ds(4 * core, 4)], local_sem.at[2]),
        pltpu.make_async_copy(flux_hbm, small.at[core], local_sem.at[3]),
    ]
    for copy in local:
        copy.start()

    swaps = [
        pltpu.make_async_remote_copy(
            src_ref=src, dst_ref=dst, send_sem=swap_send.at[i], recv_sem=swap_recv.at[i],
            device_id=partner, device_id_type=MESH,
        )
        for i, (src, dst) in enumerate((
            (k_hbm.at[:, 1 - core], buf.at[:, pl.ds(4 * core, 4)]),
            (flux_hbm, small.at[core]),
        ))
    ]
    halos = [
        [
            pltpu.make_async_remote_copy(
                src_ref=x_hbm.at[pl.ds(fl * LEVELS, LEVELS), row], dst_ref=halo.at[d, pl.ds(fl * LEVELS, LEVELS)],
                send_sem=halo_send.at[d, fl], recv_sem=halo_recv.at[d, fl],
                device_id=(peer, c), device_id_type=MESH,
            )
            for fl in range(FIELDS)
        ]
        for d, row, peer in ((0, 1, up), (1, 0, down))
    ]

    @pl.when(core == 0)
    def _():
        pl.semaphore_wait(barrier, 5)
        pl.semaphore_signal(near_sem, inc=1, device_id=partner, device_id_type=MESH)

    @pl.when(core == 1)
    def _():
        pl.semaphore_wait(near_sem, 1)

    for pair in zip(halos[0][:AHEAD], halos[1][:AHEAD]):
        for copy in pair:
            copy.start()
    for copy in swaps:
        copy.start()

    @pl.when(y < 2)
    def _():
        for n in range(2):
            halos[n][2].start()

    @pl.when(core == 1)
    def _():
        pl.semaphore_wait(barrier, 2 * (FACES - 1 + 3) + 1)
        for peer in y_peers + [(pf, pc ^ 1) for pf, pc in y_peers] + [partner]:
            pl.semaphore_signal(go_sem, inc=1, device_id=peer, device_id_type=MESH)

    lane = lax.broadcasted_iota(jnp.int32, (8, LANES), 1)
    sub = lax.broadcasted_iota(jnp.int32, (8, LANES), 0)
    local[0].wait()
    x_rows = xin.reshape(FIELDS * LEVELS * 2, LANES)

    def pack(fl, edges):
        edges = list(edges)
        for j in range(STEPS):
            i = fl * STEPS + j
            for r in range(2):
                p = x_rows[pl.ds(fl * 2 * LEVELS + 2 * j + r, BLOCKS, stride=2 * STEPS), :]
                packed[r, fl, j] = p
                edges[r] = jnp.where(lane == i, pltpu.roll(p, i + 1, axis=1), edges[r])
                edges[2 + r] = jnp.where(lane == i, pltpu.roll(p, i, axis=1), edges[2 + r])
        return tuple(edges)

    edges = lax.fori_loop(0, FIELDS, pack, tuple(jnp.zeros((8, LANES), F32) for _ in range(4)))
    for n in range(4):
        edge_out[n // 2, n % 2] = edges[n]

    local[2].wait()
    local[3].wait()
    for copy in swaps:
        copy.wait_recv()
    high = (lax.broadcasted_iota(jnp.int32, (1, LANES), 1) & 4) != 0
    for g in range(4):
        first, second = small[0, g], small[1, g]
        both = jnp.where(
            core == 0,
            jnp.where(high, pltpu.roll(second, 4, axis=1), first),
            jnp.where(high, second, pltpu.roll(first, LANES - 4, axis=1)),
        )
        buf[pl.ds(16 * g, 16), 8] = jnp.broadcast_to(both, (16, 1, LANES))

    def send(pf, py):
        pltpu.make_async_remote_copy(
            src_ref=buf.at[pf * 4 + py], dst_ref=recv.at[chip], send_sem=all_send, recv_sem=all_recv,
            device_id=(pf, py * 2 + core), device_id_type=MESH,
        ).start()

    @pl.when(core == 1)
    def _():
        pl.semaphore_wait(go_sem, len(y_peers))

    @pl.when(core == 0)
    def _():
        pl.semaphore_wait(go_sem, len(y_peers) + 1)

    for i in range(1, CHIPS):
        send((f + (i >> 2)) & 15, (y + (i & 3)) & 3)

    @pl.when(jnp.logical_not(y < 2))
    def _():
        for n in range(2):
            halos[n][2].start()

    for pair in zip(halos[0][AHEAD + 1:], halos[1][AHEAD + 1:]):
        for copy in pair:
            copy.start()
    own = pltpu.make_async_copy(buf.at[chip], recv.at[chip], local_sem.at[4])
    own.start()
    edge_copies = [
        pltpu.make_async_remote_copy(
            src_ref=edge_out.at[n], dst_ref=edge_in.at[n], send_sem=edge_send.at[n], recv_sem=edge_recv.at[n],
            device_id=(f, (c + step) & 7), device_id_type=MESH,
        )
        for n, step in ((0, 1), (1, 7))
    ]
    for copy in edge_copies:
        copy.start()

    local[1].wait()
    t = target[...]
    owner_hot = (lax.broadcasted_iota(jnp.int32, (FACES * COLS, 256), 0) == t).astype(F32)
    before = (
        lax.broadcasted_iota(jnp.int32, (256, 256), 0) < lax.broadcasted_iota(jnp.int32, (256, 256), 1)
    ).astype(F32)
    running = jnp.dot(owner_hot.astype(BF16), before.astype(BF16), preferred_element_type=F32)
    rank = jnp.sum(owner_hot * running, axis=0, keepdims=True)
    row = ((t >> 1) * ROWS + (t & 1) * 4).astype(F32) + rank
    slots = lax.broadcasted_iota(jnp.int32, (CHIPS * ROWS, 256), 0).astype(F32)
    hot[...] = (slots == row).astype(F32).astype(BF16)

    for copy in edge_copies:
        copy.wait_recv()

    def smooth(fl, carry):
        for j in range(STEPS):
            i = fl * STEPS + j
            for r in range(2):
                p = packed[r, fl, j]
                left = jnp.where(lane == 0, pltpu.roll(edge_in[0, r], LANES - i, axis=1), pltpu.roll(p, 1, axis=1))
                right = jnp.where(
                    lane == LANES - 1,
                    pltpu.roll(edge_in[1, r], LANES - 1 - i, axis=1),
                    pltpu.roll(p, LANES - 1, axis=1),
                )
                base[r, fl, j] = SMOOTHING * (packed[1 - r, fl, j] + left + right - 4.0 * p)
        return carry

    lax.fori_loop(0, FIELDS, smooth, 0)

    own.wait()
    pltpu.make_async_copy(recv.at[pl.ds(0, CHIPS - 1)], recv.at[pl.ds(0, CHIPS - 1)], all_recv).wait()
    received = recv.reshape(CHIPS * ROWS, LANES)
    columns = lookup(received[...], hot[...])
    kappa_t[0] = columns[:, :LANES]
    kappa_t[1] = columns[:, LANES:]
    flux_hot = (lax.broadcasted_iota(jnp.int32, (CHIPS, 256), 0) == (t >> 1)).astype(F32)
    flux = lookup(received[pl.ds(8, CHIPS, stride=ROWS), :], flux_hot.astype(BF16))
    wanted = rank + ((t & 1) * 4 + ((f & 3) * 32 + y * 8)).astype(F32)
    lanes_at = lax.broadcasted_iota(jnp.int32, (LANES, 256), 0).astype(F32)
    heat = jnp.sum(jnp.where(lanes_at == wanted, flux, 0.0), axis=0, keepdims=True)
    heat = [jnp.where(sub == BLOCKS - 1, heat[:, r * LANES : (r + 1) * LANES], 0.0) for r in range(2)]

    def interface(j):
        return jnp.stack([kappa_t[r, pl.ds(j, BLOCKS, stride=STEPS), :] for r in range(2)])

    subs = jnp.stack([sub, sub])
    ks = [interface(j) for j in range(STEPS)]
    last = jnp.where(subs == BLOCKS - 1, 0.0, ks[-1])
    above = jnp.where(subs == 0, 0.0, pltpu.roll(ks[-1], 1, axis=1))
    q = 1.0 + above
    u = above
    d = packed[:, :, 0]
    work[:, :, 0] = d
    us, rps, gs = [u], [], []
    for j in range(1, STEPS + 1):
        k = ks[j - 1]
        pivot = q + k
        if j == STEPS:
            break
        rp = 1.0 / pivot
        g = k * rp
        q = 1.0 + (k * q) * rp
        d = packed[:, :, j] + g[:, None] * d
        u = g * u
        if j == STEPS - 1:
            d = jnp.concatenate([(d[:, :1] + jnp.stack(heat)[:, None]), d[:, 1:]], axis=1)
        else:
            work[:, :, j] = d
        us.append(u)
        rps.append(rp)
        gs.append(g)
    v = rps[-1][:, None] * work[:, :, STEPS - 2]
    w = gs[-1]
    u0 = rps[-1] * us[STEPS - 2]
    work[:, :, STEPS - 2] = v
    u_all, w_all = [None] * STEPS, [None] * STEPS
    u_all[STEPS - 2], w_all[STEPS - 2] = u0, w
    for j in range(STEPS - 3, -1, -1):
        v = rps[j][:, None] * work[:, :, j] + gs[j][:, None] * v
        u0 = rps[j] * us[j] + gs[j] * u0
        w = gs[j] * w
        work[:, :, j] = v
        u_all[j], w_all[j] = u0, w

    def prev(value, n=1):
        return pltpu.roll(value, n, axis=value.ndim - 2)

    def following(value, n=1):
        return pltpu.roll(value, BLOCKS - n, axis=value.ndim - 2)

    inverse = 1.0 / (pivot - last * following(u0))
    a = us[STEPS - 1] * inverse
    b = last * following(w) * inverse
    rhs = (d + last[:, None] * following(v)) * inverse[:, None]
    for n in (1, 2, 4):
        inverse = 1.0 / (1.0 - a * prev(b, n) - b * following(a, n))
        rhs = (rhs + a[:, None] * prev(rhs, n) + b[:, None] * following(rhs, n)) * inverse[:, None]
        a, b = a * prev(a, n) * inverse, b * following(b, n) * inverse
    bottom = rhs
    top = jnp.where(subs[:, None] == 0, 0.0, prev(bottom))
    for j in range(STEPS - 1):
        base[:, :, j] += work[:, :, j] + u_all[j][:, None] * top + w_all[j][:, None] * bottom
    base[:, :, STEPS - 1] += bottom

    halo_rows = halo.reshape(2 * FIELDS * LEVELS, LANES)
    out_rows = out.reshape(FIELDS * LEVELS * 2, LANES)
    for fl in range(FIELDS):
        for d_at in range(2):
            halos[d_at][fl].wait_recv()
        for j in range(STEPS):
            for r in range(2):
                beside = halo_rows[pl.ds((r * FIELDS + fl) * LEVELS + j, BLOCKS, stride=STEPS), :]
                out_rows[pl.ds(fl * 2 * LEVELS + 2 * j + r, BLOCKS, stride=2 * STEPS), :] = (
                    base[r, fl, j] + SMOOTHING * beside
                )
    pltpu.make_async_copy(recv.at[pl.ds(0, CHIPS - 1)], recv.at[pl.ds(0, CHIPS - 1)], all_send).wait()
    for copy in swaps + edge_copies + halos[0] + halos[1]:
        copy.wait_send()


def shards(prognostic, diffusivity, surface_flux, assignment):
    x = prognostic.reshape(FIELDS * LEVELS, 2, 1, LANES)
    k = diffusivity.reshape(CHIPS, 2, 4, 1, LEVELS)
    flux = surface_flux.reshape(4, 1, LANES)
    target = assignment.reshape(1, 256)
    any_spec = pl.BlockSpec(memory_space=pl.ANY)
    dma = pltpu.SemaphoreType.DMA
    wide = (2, FIELDS, STEPS, BLOCKS, LANES)
    result = pl.pallas_call(
        kernel,
        out_shape=pltpu.VMEM(x.shape, F32),
        name="exchange",
        in_specs=[any_spec] * 4,
        out_specs=pl.BlockSpec(memory_space=pltpu.VMEM),
        scratch_shapes=[
            pltpu.VMEM(x.shape, F32),
            pltpu.VMEM((1, 256), jnp.int32),
            pltpu.VMEM((2, 4, 1, LANES), F32),
            pltpu.VMEM((CHIPS, ROWS, 1, LANES), F32),
            pltpu.VMEM((CHIPS, ROWS, 1, LANES), F32),
            pltpu.VMEM((2, FIELDS * LEVELS, 1, LANES), F32),
            pltpu.VMEM(wide, F32),
            pltpu.VMEM(wide, F32),
            pltpu.VMEM(wide, F32),
            pltpu.VMEM((2, 2, BLOCKS, LANES), F32),
            pltpu.VMEM((2, 2, BLOCKS, LANES), F32),
            pltpu.VMEM((CHIPS * ROWS, 256), BF16),
            pltpu.VMEM((2, LEVELS, LANES), F32),
            dma((5,)),
            dma((2,)),
            dma((2,)),
            dma((2, FIELDS)),
            dma((2, FIELDS)),
            dma((2,)),
            dma((2,)),
            dma,
            dma,
            pltpu.SemaphoreType.REGULAR,
            pltpu.SemaphoreType.REGULAR,
        ],
        compiler_params=pltpu.CompilerParams(
            collective_id=0, has_side_effects=True, vmem_limit_bytes=56 << 20
        ),
    )(x, k, flux, target)
    return result.reshape(prognostic.shape)


def solution(mesh):
    return jax.shard_map(
        shards,
        mesh=mesh,
        in_specs=(
            P(None, None, "face", "col"),
            P("face", "col", None, None),
            P("face", "col", None),
            P("face", "col", None, None),
        ),
        out_specs=P(None, None, "face", "col"),
        check_vma=False,
    )
```
